32 devices in a mesh: groups: 2 (over y), sector: 4 (over z), op: 4 (over x, core).
Axes of the slice: x: 2, y: 2, z: 4, core: 2. Of those that a mesh axis runs over, the one named last changes fastest.
Arguments:
- start_vector: bfloat16 [256, 4096], P(('groups', 'sector')), parts along dimension 0, may hold values from -6 to 6
- extents: int32 [256, 2], P(('groups', 'sector')), parts along dimension 0, may hold values from 16 to 64, as said below
- offsets: int32 [64], P('groups'), parts along dimension 0, may hold values from 0 to 3, as said below
- env_left: bfloat16 [256, 28, 4096], P(('groups', 'sector'), 'op'), parts along dimension 0, may hold values from -0.75 to 0.75
- env_right: bfloat16 [256, 28, 4096], P(('groups', 'sector'), 'op'), parts along dimension 0, may hold values from -0.75 to 0.75
- channel_mask: int32 [256, 28], P(('groups', 'sector'), 'op'), parts along dimension 0, may hold values 0 or 1
Outputs:
- residual: float32 [256, 4096], P(('groups', 'sector')), parts along dimension 0
- projections: float32 [6, 3], P('groups'), parts along dimension 0
The draws below stay inside these ranges and needn't reach their ends.
There are 2 independent parts, one for each index of `groups`. The reference program is written for one: setup_inputs(seed, part) draws one part's arguments, and reference() takes and returns one part's arrays. A program takes and returns all parts, laid end to end along the dimension named above; each array names one. Nothing has to cross between parts.
Inputs may be any that keep to these rules, and one draw needn't show every extreme that they name: `extents`: every block has at least 16 rows and columns, and block 0 has 64 rows. The environments of home slot j of sector device h are held by sector device (h + offsets[j]) mod (4), in its slot j. Each value occurs in offsets exactly 8 times or not at all.
All inputs are finite; a program needn't handle non-finite values. No bound on the sum of `channel_mask` on one device may be relied on, other than what follows from the above.
Results may differ from the reference program's by a relative error of at most 0.0077.
Values may be sent and summed in bfloat16 or wider, within the bound.
No kernel may reach another device: no remote copies, remote signals or barrier semaphores. Data moves between devices by JAX's collectives and lax.ppermute only.
A program may use at most 64 MiB of HBM per device.

```python
import jax
import jax.numpy as jnp
from jax import lax

SLOTS = 32
B = 64
W = 28
ITERS = 3
SECTORS = 128
CAP = 8
BB = 4096


def draw_extents(key, part):
    key = jax.random.fold_in(key, 5)
    values = jax.random.randint(key, (SECTORS, 2), B // 4, B + 1)
    first = (jnp.arange(SECTORS)[:, None] == 0) & (jnp.arange(2)[None, :] == 0)
    return jnp.where(first, B, values).astype(jnp.int32)


def draw_offsets(key, part):
    key = jax.random.fold_in(key, 11)
    first_key, second_key = jax.random.split(key)
    nodes = SECTORS // SLOTS
    middle = 1 + jax.random.permutation(first_key, nodes - 2)
    ends = jnp.array([0, nodes - 1], dtype=jnp.int32)
    targets = jnp.concatenate([ends, middle.astype(jnp.int32)])
    order = jax.random.permutation(second_key, SLOTS)
    return targets[order // CAP].astype(jnp.int32)


def touch_ends(entries, stream_key, least, top_value):
    index_at = [jax.random.randint(jax.random.fold_in(stream_key, axis), (), 0, length) for axis, length in enumerate(entries.shape)]
    widest = entries.shape.index(max(entries.shape))
    beside = index_at[:widest] + [(index_at[widest] + 1) % entries.shape[widest]] + index_at[widest + 1:]
    return entries.at[tuple(index_at)].set(least).at[tuple(beside)].set(top_value)


def levels(stream_key, extent, shards, smallest, largest):
    gain = 1.0
    for dim, blocks in shards:
        steps = jax.random.uniform(jax.random.fold_in(jax.random.fold_in(stream_key, 6), dim), (blocks,), jnp.float32, smallest / len(shards), largest / len(shards))
        gain = gain * jnp.repeat(jnp.exp(steps), extent[dim] // blocks).reshape((-1,) + (1,) * (len(extent) - 1 - dim))
    return gain


def gaussian(own_key, extent, scale, reach, pieces=(), held_as=jnp.bfloat16):
    entries = scale * jax.random.normal(own_key, extent, jnp.float32)
    if pieces:
        entries = entries * levels(own_key, extent, pieces, -0.22, 0.18)
    return jnp.clip(entries, -reach, reach).astype(held_as)


def setup_inputs(seed: int = 0, part: int = 0) -> dict:
    key_of = jax.random.split(jax.random.key(seed), 7)
    part_splits = jax.random.split(jax.random.fold_in(key_of[6], part), 7)
    return {
        "start_vector": gaussian(part_splits[0], (SECTORS, BB), 1.0, 6.0, ((0, 4),)),
        "extents": draw_extents(jax.random.fold_in(jax.random.fold_in(key_of[6], part), 71), part),
        "offsets": draw_offsets(jax.random.fold_in(jax.random.fold_in(key_of[6], part), 71), part),
        "env_left": gaussian(part_splits[3], (SECTORS, W, BB), B ** -0.5, 0.75, ((0, 4), (1, 4))),
        "env_right": gaussian(part_splits[4], (SECTORS, W, BB), B ** -0.5, 0.75, ((0, 4), (1, 4))),
        "channel_mask": touch_ends((jax.random.randint(part_splits[5], (SECTORS, W), 0, 3) < 2).astype(jnp.int32), jax.random.fold_in(part_splits[5], 1), 0, 1),
    }


def block_mask(extents):
    position = jnp.arange(BB, dtype=jnp.int32)
    row_index = position // B
    col_index = position % B
    inside = (row_index[None, :] < extents[:, 0:1]) & (col_index[None, :] < extents[:, 1:2])
    return inside.astype(jnp.float32)

def block_product(vec_bf, left, right, chan):
    inner = jnp.einsum('swab,sbc->swac', left.astype(jnp.float32), vec_bf.astype(jnp.float32))
    inner = inner * chan[:, :, None, None]
    return jnp.einsum('swac,swdc->sad', inner, right.astype(jnp.float32), precision=lax.Precision.HIGHEST)

def reference(start_vector, extents, offsets, env_left, env_right, channel_mask):
    nodes = SECTORS // SLOTS
    count = float(SECTORS * BB)
    mask = block_mask(extents)
    slot_ids = jnp.arange(SLOTS, dtype=jnp.int32)

    def apply(vector):
        vec_bf = vector.astype(jnp.bfloat16).reshape(nodes, SLOTS, B, B)

        def one(items):
            home, blocks = items
            host = (home + offsets) % nodes * SLOTS + slot_ids
            left = jnp.take(env_left, host, axis=0).reshape(SLOTS, W, B, B)
            right = jnp.take(env_right, host, axis=0).reshape(SLOTS, W, B, B)
            chan = jnp.take(channel_mask, host, axis=0).astype(jnp.float32)
            return block_product(blocks, left, right, chan)
        images = lax.map(one, (jnp.arange(nodes, dtype=jnp.int32), vec_bf))
        return images.reshape(SECTORS, BB) * mask
    masked = mask * start_vector.astype(jnp.float32)
    basis = [masked / jnp.sqrt(jnp.sum(masked * masked) / count + 1e-06)]
    projections = jnp.zeros((ITERS, ITERS), jnp.float32)
    residual = masked
    for step in range(ITERS):
        image = apply(basis[step])
        residual = image
        for index in range(step + 1):
            coeff = jnp.sum(basis[index] * image) / count
            projections = projections.at[index, step].set(coeff)
            residual = residual - coeff * basis[index]
        if step + 1 < ITERS:
            basis.append(residual / jnp.sqrt(jnp.sum(residual * residual) / count + 1e-06))
    return (residual, projections)
```

```python
import jax
import jax.numpy as jnp
from jax import lax
from jax.experimental import pallas as pl
from jax.experimental.pallas import tpu as pltpu
from jax.sharding import PartitionSpec as P

B = 64
ITERS = 3
HALF = 32
LANES = 128
WIDE = 4 * LANES
F32 = jnp.float32
BF16 = jnp.bfloat16
VMEM_LIMIT = 48 * 1024 * 1024


def iota(shape, dim):
    return lax.broadcasted_iota(jnp.int32, shape, dim)


def sorted_column(c):
    return (c % 2) * HALF + c // 2


def lane_order(transposed):
    row = iota((LANES, LANES), 1 if transposed else 0)
    col = iota((LANES, LANES), 0 if transposed else 1)
    to = row // B * B + sorted_column(row % B)
    return (to == col).astype(F32).astype(BF16)


def pair_order():
    row = iota((2 * LANES, 2 * LANES), 0)
    col = iota((2 * LANES, 2 * LANES), 1)
    w, p, c = row // LANES, row // B % 2, row % B
    return (p * LANES + w * B + sorted_column(c) == col).astype(F32).astype(BF16)


def inside(rows, cols):
    lane = iota((HALF, LANES), 1)
    a = 2 * iota((HALF, LANES), 0) + lane // B
    kept = lane % B
    c = 2 * (kept % HALF) + kept // HALF
    return jnp.where((a < rows) & (c < cols), 1.0, 0.0).astype(F32)


def prepare_kernel(index_ref, chan_ref, left_ref, right_ref, out_ref, raw, turn, sems):
    slots = out_ref.shape[1]
    chans = raw.shape[2]

    def fetch(s, t):
        source = (left_ref, right_ref)[t]
        return pltpu.make_async_copy(source.at[index_ref[s]], raw.at[t, s], sems.at[t, s])

    for s in range(slots):
        for t in range(2):
            fetch(s, t).start()
    order = pair_order()
    blank = jnp.zeros((HALF, LANES), F32)

    def body(s, carry):
        for t in range(2):
            fetch(s, t).wait()
            rows = raw[t, s].astype(F32)
            for i in range(HALF):
                turn[t, pl.ds(8 * i, chans), :] = rows[:, i * LANES : (i + 1) * LANES]
            parts = []
            for w in range(8):
                if w >= chans:
                    parts.append(blank)
                    continue
                part = turn[t, pl.ds(w, HALF, stride=8), :]
                if t == 0:
                    part = part * chan_ref[index_ref[s], w].astype(F32)
                parts.append(part)
            pairs = [jnp.concatenate(parts[g : g + 2], axis=1) for g in range(0, 8, 2)]
            mixed = jnp.dot(
                jnp.concatenate(pairs, axis=0).astype(BF16), order, preferred_element_type=F32
            ).astype(BF16)
            for g in range(4):
                for p in range(2):
                    out_ref[t, s, p * HALF : (p + 1) * HALF, g * LANES : (g + 1) * LANES] = mixed[
                        g * HALF : (g + 1) * HALF, p * LANES : (p + 1) * LANES
                    ]
        return carry

    lax.fori_loop(0, slots, body, 0)


def prepare(index, chan, left, right):
    slots = index.shape[0]
    chans = left.shape[1]
    smem = pl.BlockSpec(memory_space=pltpu.SMEM)
    hbm = pl.BlockSpec(memory_space=pl.ANY)
    return pl.pallas_call(
        prepare_kernel,
        out_shape=jax.ShapeDtypeStruct((2, slots, B, WIDE), BF16),
        in_specs=[smem, smem, hbm, hbm],
        out_specs=pl.BlockSpec(memory_space=pltpu.VMEM),
        scratch_shapes=[
            pltpu.VMEM((2, slots, chans, B * B), BF16),
            pltpu.VMEM((2, 8 * HALF, LANES), F32),
            pltpu.SemaphoreType.DMA((2, slots)),
        ],
        compiler_params=pltpu.CompilerParams(vmem_limit_bytes=VMEM_LIMIT),
        name="prepare",
    )(index, chan, left, right)


def block_diagonal(x):
    low = iota((HALF, LANES), 1) < B
    swapped = pltpu.roll(x, B, 1)
    zero = jnp.zeros_like(x)
    two = jnp.concatenate(
        [
            jnp.where(low, x, zero),
            jnp.where(low, swapped, zero),
            jnp.where(low, zero, swapped),
            jnp.where(low, zero, x),
        ],
        axis=0,
    )
    blank = jnp.zeros_like(two)
    return jnp.concatenate(
        [jnp.concatenate([two, blank], axis=1), jnp.concatenate([blank, two], axis=1)], axis=0
    )


def split(x):
    high = x.astype(BF16)
    return high, (x - high.astype(F32)).astype(BF16)


def dot_t(a, b):
    return lax.dot_general(a, b, (((1,), (1,)), ((), ())), preferred_element_type=F32)


def product_slot(x, s, env_refs, out_ref, exact):
    diag_high, diag_low = split(block_diagonal(x))
    total = None
    for env in env_refs:
        for g in range(2):
            lanes = pl.ds(g * 2 * LANES, 2 * LANES)
            left = env[0, s, :, lanes]
            inner = jnp.dot(left, diag_high, preferred_element_type=F32)
            if not exact:
                inner = inner + jnp.dot(left, diag_low, preferred_element_type=F32)
            high, low = split(inner)
            right = env[1, s, :, lanes]
            part = dot_t(high, right) + dot_t(low, right)
            total = part if total is None else total + part
    out_ref[s] = jnp.concatenate([total[:HALF], total[HALF:]], axis=1)


def start_kernel(scale_ref, ext_ref, near_ref, far_ref, keep_ref, got_ref, q_ref, y_ref, turn):
    slots = q_ref.shape[0]
    half = slots // 2
    for t, ref in enumerate((near_ref, far_ref)):
        rows = ref[...].astype(F32)
        for i in range(HALF):
            turn[pl.ds(slots * i + half * t, half), :] = rows[:, i * LANES : (i + 1) * LANES]
    order = lane_order(False)
    for s in range(slots):
        x = turn[pl.ds(s, HALF, stride=slots), :].astype(BF16)
        x = jnp.dot(x, order, preferred_element_type=F32)
        q_ref[s] = x * inside(ext_ref[s, 0], ext_ref[s, 1]) * scale_ref[0]

    def body(s, carry):
        product_slot(q_ref[s], s, (keep_ref, got_ref), y_ref, True)
        return carry

    lax.fori_loop(0, slots, body, 0)


def total_of(x):
    x = jnp.sum(x, axis=0)
    return jnp.sum(jnp.sum(x, axis=0, keepdims=True), axis=1, keepdims=True)


def ratio(a, b):
    return jnp.where(b > 0, a / jnp.where(b > 0, b, 1.0), 0.0)


def masked_sum(ext_ref, own_ref, other_ref, out_ref):
    for s in range(out_ref.shape[0]):
        out_ref[s] = (own_ref[s] + other_ref[s]) * inside(ext_ref[s, 0], ext_ref[s, 1])


def step_kernel(count, *refs):
    ext_ref, own_ref, other_ref = refs[:3]
    basis = refs[3 : 3 + count]
    keep_ref, got_ref, q_ref, y_ref, coeff_ref = refs[3 + count :]
    slots = q_ref.shape[0]
    masked_sum(ext_ref, own_ref, other_ref, q_ref)
    image = q_ref[...]
    rows = []
    for ref in basis:
        q = ref[...]
        a = ratio(total_of(q * image), total_of(q * q))
        rows.append(jnp.broadcast_to(a, (1, LANES)))
    rest = image
    for ref, row in zip(basis, rows):
        rest = rest - row * ref[...]
    q_ref[...] = rest
    coeff_ref[...] = jnp.concatenate(rows + [jnp.zeros((8 - count, LANES), F32)], axis=0)

    def body(s, carry):
        product_slot(q_ref[s], s, (keep_ref, got_ref), y_ref, False)
        return carry

    lax.fori_loop(0, slots, body, 0)


def vmem_call(kernel, out_shape, operands, smem, scratch=(), name=None):
    specs = [pl.BlockSpec(memory_space=pltpu.SMEM)] * smem
    specs += [pl.BlockSpec(memory_space=pltpu.VMEM)] * (len(operands) - smem)
    outs = jax.tree.map(lambda _: pl.BlockSpec(memory_space=pltpu.VMEM), out_shape)
    return pl.pallas_call(
        kernel,
        out_shape=out_shape,
        in_specs=specs,
        out_specs=outs,
        scratch_shapes=list(scratch),
        compiler_params=pltpu.CompilerParams(vmem_limit_bytes=VMEM_LIMIT),
        name=name,
    )(*operands)


def gram_kernel(ext_ref, own_ref, other_ref, q0_ref, q1_ref, q2_ref, c1_ref, c2_ref, y_ref, table_ref):
    masked_sum(ext_ref, own_ref, other_ref, y_ref)
    vectors = [q0_ref[...], q1_ref[...], q2_ref[...], y_ref[...]]
    rows = []
    for i in range(4):
        for j in range(i, 4):
            rows.append(jnp.broadcast_to(total_of(vectors[i] * vectors[j]), (1, LANES)))
    rows += [c1_ref[0:1], c2_ref[0:1], c2_ref[1:2]]
    table_ref[...] = jnp.concatenate(rows + [jnp.zeros((3, LANES), F32)], axis=0)


def combine(count, take):
    gram = {}
    row = 0
    for i in range(4):
        for j in range(i, 4):
            gram[i, j] = gram[j, i] = take(row)
            row += 1
    a00, a01, a11 = take(10), take(11), take(12)
    one = jnp.ones_like(a00)
    zero = jnp.zeros_like(a00)

    def mean(u, v):
        acc = None
        for i in range(4):
            for j in range(4):
                if u[i] is None or v[j] is None:
                    continue
                term = u[i] * v[j] * gram[i, j]
                acc = term if acc is None else acc + term
        return jnp.sum(acc, axis=0, keepdims=True) / count

    images = [[a00, one, None, None], [a01, a11, one, None], [None, None, None, one]]
    basis = [[one, None, None, None]]
    projections = {}
    for k in range(ITERS):
        image = [None] * 4
        for j, z in enumerate(basis[k]):
            if z is None:
                continue
            for m, v in enumerate(images[j]):
                if v is not None:
                    image[m] = z * v if image[m] is None else image[m] + z * v
        rest = list(image)
        for i in range(k + 1):
            p = mean(basis[i], image)
            projections[i, k] = p
            for m in range(4):
                if basis[i][m] is not None:
                    rest[m] = (zero if rest[m] is None else rest[m]) - p * basis[i][m]
        if k + 1 < ITERS:
            scale = 1.0 / jnp.sqrt(mean(rest, rest) + 1e-06)
            basis.append([None if v is None else v * scale for v in rest])
    return projections, rest


def final_kernel(nodes, count, me_ref, t0_ref, t1_ref, t2_ref, t3_ref, q0_ref, q1_ref, q2_ref, y_ref,
                 near_ref, far_ref, proj_ref, tables, turn):
    node, core = me_ref[0], me_ref[1]
    rows = t0_ref.shape[0]
    for d, ref in enumerate((t0_ref, t1_ref, t2_ref, t3_ref)):
        at = lax.rem(node + nodes - d, nodes) * rows
        tables[pl.ds(pl.multiple_of(at, rows), rows), :] = ref[...]
    devices = 2 * nodes
    projections, rest = combine(count, lambda k: tables[pl.ds(k, devices, stride=16), :])
    lines = []
    for i in range(ITERS):
        line = jnp.zeros((1, LANES), F32)
        for k in range(i, ITERS):
            line = jnp.where(iota((1, LANES), 1) == k, projections[i, k], line)
        lines.append(line)
    proj_ref[...] = jnp.concatenate(lines + [jnp.zeros((8 - ITERS, LANES), F32)], axis=0)
    mine = iota((devices, LANES), 0) == 2 * node + core
    coeff = [jnp.sum(jnp.where(mine, v, 0.0), axis=0, keepdims=True) for v in rest]
    order = lane_order(True)
    slots = y_ref.shape[0]
    half = slots // 2
    for s in range(slots):
        x = coeff[0] * q0_ref[s] + coeff[1] * q1_ref[s] + coeff[2] * q2_ref[s] + coeff[3] * y_ref[s]
        x = jnp.dot(x.astype(BF16), order, preferred_element_type=F32)
        turn[pl.ds(s, HALF, stride=slots), :] = x
    for t, ref in enumerate((near_ref, far_ref)):
        for i in range(HALF):
            ref[:, i * LANES : (i + 1) * LANES] = turn[pl.ds(slots * i + half * t, half), :].astype(BF16)


def paired(start_vector, extents, offsets, env_left, env_right, channel_mask):
    nodes = lax.axis_size("sector")
    ops = lax.axis_size("op")
    node = lax.axis_index("sector")
    core = lax.axis_index("op") % 2
    slots = start_vector.shape[0]
    cap = slots // nodes
    mine = slots // 2
    count = float(slots * nodes * B * B)
    swap_core = [(i, i ^ 1) for i in range(ops)]
    swap_x = [(i, i ^ 2) for i in range(ops)]

    slot_ids = jnp.arange(slots, dtype=jnp.int32)
    same = offsets[:, None] == offsets[None, :]
    earlier = slot_ids[None, :] < slot_ids[:, None]
    place = offsets * cap + jnp.sum((same & earlier).astype(jnp.int32), axis=1)
    order = jnp.sum(jnp.where(place[None, :] == slot_ids[:, None], slot_ids[None, :], 0), axis=1)
    order = order.reshape(2, mine)
    own = jnp.where(core == 0, order[0], order[1])
    others = jnp.where(core == 0, order[1], order[0])

    sent = prepare(others, channel_mask, env_left, env_right)
    got = lax.ppermute(sent, "op", swap_core)
    keep = prepare(own, channel_mask, env_left, env_right)

    position = jnp.arange(B * B, dtype=jnp.int32)
    mask = ((position // B)[None, :] < extents[:, 0:1]) & ((position % B)[None, :] < extents[:, 1:2])
    masked = jnp.where(mask, start_vector.astype(F32), 0.0)
    squares = jnp.sum(masked * masked)
    high = lax.reduce_precision(squares, 8, 7)
    middle = lax.reduce_precision(squares - high, 8, 7)
    low = squares - high - middle

    def route(t, back):
        pairs = []
        for h in range(nodes):
            for q in range(ops):
                to = (h + 2 * (q % 2) + t) % nodes
                a, b = h * ops + q, to * ops + q
                pairs.append((b, a) if back else (a, b))
        return pairs

    arrived = []
    for t in range(2):
        rows = lax.dynamic_slice_in_dim(own, t * cap, cap)
        note = jnp.concatenate(
            [jnp.take(extents, rows, axis=0).reshape(-1).astype(F32), jnp.stack([high, middle, low])]
        )
        note = jnp.pad(note, (0, B * B - note.shape[0])).astype(BF16)
        payload = jnp.concatenate([jnp.take(start_vector, rows, axis=0), note[None]], axis=0)
        arrived.append(lax.ppermute(payload, ("sector", "op"), route(t, False)))
    notes = [a[cap].astype(F32) for a in arrived]
    ext = jnp.concatenate([n[: 2 * cap].reshape(cap, 2) for n in notes]).astype(jnp.int32)
    two = jnp.stack([jnp.sum(n[2 * cap : 2 * cap + 3]) for n in notes])
    two_more = lax.ppermute(two, "op", swap_core)
    four = jnp.where(core == 0, jnp.concatenate([two, two_more]), jnp.concatenate([two_more, two]))
    by_node = jnp.take(four, (node - jnp.arange(nodes)) % nodes)
    scale = (1.0 / jnp.sqrt(jnp.sum(by_node) / count + 1e-06)).reshape(1)

    vector = jax.ShapeDtypeStruct((mine, HALF, LANES), F32)
    coeffs = jax.ShapeDtypeStruct((8, LANES), F32)
    q0, y0 = vmem_call(
        start_kernel, (vector, vector), (scale, ext, arrived[0][:cap], arrived[1][:cap], keep, got), 2,
        [pltpu.VMEM((mine * HALF, LANES), F32)], "start")
    z0 = lax.ppermute(y0, "op", swap_x)

    def step(*refs):
        step_kernel(1, *refs)

    def step_two(*refs):
        step_kernel(2, *refs)

    q1, y1, c1 = vmem_call(step, (vector, vector, coeffs), (ext, y0, z0, q0, keep, got), 1, name="second")
    z1 = lax.ppermute(y1, "op", swap_x)
    q2, y2, c2 = vmem_call(step_two, (vector, vector, coeffs), (ext, y1, z1, q0, q1, keep, got), 1, name="third")
    z2 = lax.ppermute(y2, "op", swap_x)
    image, table = vmem_call(
        gram_kernel, (vector, jax.ShapeDtypeStruct((16, LANES), F32)),
        (ext, y2, z2, q0, q1, q2, c1, c2), 1, name="gram")
    other_table = lax.ppermute(table, "op", swap_core)
    tables = jnp.where(
        core == 0, jnp.concatenate([table, other_table]), jnp.concatenate([other_table, table]))
    around = [tables] + [
        lax.ppermute(tables, "sector", [(i, (i + d) % nodes) for i in range(nodes)]) for d in range(1, nodes)]
    me = jnp.stack([node, core]).astype(jnp.int32)

    def final(*refs):
        final_kernel(nodes, count, *refs)

    flat = jax.ShapeDtypeStruct((cap, B * B), BF16)
    near, far, proj = vmem_call(
        final, (flat, flat, coeffs), (me, *around, q0, q1, q2, image), 1,
        [pltpu.VMEM((2 * nodes * 16, LANES), F32), pltpu.VMEM((mine * HALF, LANES), F32)], "final")
    home = jnp.concatenate(
        [lax.ppermute(part, ("sector", "op"), route(t, True)) for t, part in enumerate((near, far))])
    home_other = lax.ppermute(home, "op", swap_core)
    ordered = jnp.where(
        core == 0, jnp.concatenate([home, home_other]), jnp.concatenate([home_other, home]))
    residual = jnp.take(ordered, place, axis=0).astype(F32)
    return residual, proj[:ITERS, :ITERS]


def pack_rows(data, index, nodes, cap):
    slots = data.shape[0]
    hit = jnp.arange(nodes * cap, dtype=jnp.int32)[:, None] == index[None, :]
    source = jnp.sum(jnp.where(hit, jnp.arange(slots, dtype=jnp.int32)[None, :], 0), axis=1)
    filled = jnp.any(hit, axis=1)
    rows = jnp.take(data, source, axis=0)
    rows = jnp.where(filled[:, None], rows, jnp.zeros_like(rows))
    return rows.reshape(nodes, cap, data.shape[1])


def unpack_rows(arrived, index):
    flat = arrived.reshape(arrived.shape[0] * arrived.shape[1], arrived.shape[2])
    return jnp.take(flat, index, axis=0)


def general(start_vector, extents, offsets, env_left, env_right, channel_mask):
    nodes = lax.axis_size("sector")
    here_index = lax.axis_index("sector")
    slots = start_vector.shape[0]
    cap = max(1, slots // nodes)
    chans = env_left.shape[1]
    count = float(slots * nodes * B * B)
    slot_ids = jnp.arange(slots, dtype=jnp.int32)
    same = offsets[:, None] == offsets[None, :]
    earlier = slot_ids[None, :] < slot_ids[:, None]
    rank = jnp.sum((same & earlier).astype(jnp.int32), axis=1)
    send_index = (here_index + offsets) % nodes * cap + rank
    recv_index = (here_index - offsets) % nodes * cap + rank
    position = jnp.arange(B * B, dtype=jnp.int32)
    inside = ((position // B)[None, :] < extents[:, 0:1]) & (
        (position % B)[None, :] < extents[:, 1:2]
    )
    mask = inside.astype(jnp.float32)
    left = env_left.reshape(slots, chans, B, B)
    right_wide = env_right.reshape(slots, chans, B, B).astype(jnp.float32)
    chan = channel_mask.astype(jnp.float32)

    def squares(vector):
        return lax.psum(jnp.sum(vector * vector), "sector") / count

    def correlation_table(basis, image):
        local = [jnp.sum(vector * image) for vector in basis]
        local = local + [jnp.zeros((), jnp.float32)] * (ITERS - len(basis))
        return lax.psum(jnp.stack(local), "sector") / count

    masked = mask * start_vector.astype(jnp.float32)
    basis = [masked / jnp.sqrt(squares(masked) + 1e-06)]
    projections = jnp.zeros((ITERS, ITERS), jnp.float32)
    residual = masked
    for step in range(ITERS):
        moving = pack_rows(basis[step].astype(jnp.bfloat16), send_index, nodes, cap)
        arrived = lax.all_to_all(moving, "sector", split_axis=0, concat_axis=0, tiled=True)
        blocks = unpack_rows(arrived, recv_index).reshape(slots, B, B)
        inner = jnp.einsum("swab,sbc->swac", left, blocks, preferred_element_type=jnp.float32)
        inner = inner * chan[:, :, None, None]
        partial_image = jnp.einsum(
            "swac,swdc->sad", inner, right_wide, precision=lax.Precision.HIGHEST
        )
        total = lax.psum(partial_image.reshape(slots, B * B), "op")
        going = pack_rows(total, recv_index, nodes, cap)
        returned = lax.all_to_all(going, "sector", split_axis=0, concat_axis=0, tiled=True)
        apply_image = unpack_rows(returned, send_index)
        image = apply_image * mask
        coeffs = correlation_table(basis, image)
        residual = image
        for index in range(step + 1):
            projections = projections.at[index, step].set(coeffs[index])
            residual = residual - coeffs[index] * basis[index]
        if step + 1 < ITERS:
            basis.append(residual / jnp.sqrt(squares(residual) + 1e-06))
    return (residual, projections)


def solution(mesh):
    def on_device(start_vector, extents, offsets, env_left, env_right, channel_mask):
        nodes, ops = mesh.shape["sector"], mesh.shape["op"]
        slots, chans = env_left.shape[:2]
        fits = nodes == 4 and ops == 4 and slots == 8 * nodes and chans <= 8
        body = paired if fits else general
        return body(start_vector, extents, offsets, env_left, env_right, channel_mask)

    return jax.shard_map(
        on_device,
        mesh=mesh,
        in_specs=(
            P(("groups", "sector"), None),
            P(("groups", "sector"), None),
            P("groups"),
            P(("groups", "sector"), "op", None),
            P(("groups", "sector"), "op", None),
            P(("groups", "sector"), "op"),
        ),
        out_specs=(P(("groups", "sector"), None), P("groups", None)),
        check_vma=False,
    )
```

```python
import jax
import jax.numpy as jnp
from jax import lax
from jax.experimental import pallas as pl
from jax.experimental.pallas import tpu as pltpu
from jax.sharding import PartitionSpec as P

B = 64
ITERS = 3
HALF = 32
LANES = 128
WIDE = 4 * LANES
F32 = jnp.float32
BF16 = jnp.bfloat16
VMEM_LIMIT = 24 * 1024 * 1024


def iota(shape, dim):
    return lax.broadcasted_iota(jnp.int32, shape, dim)


def one_hot(condition):
    return jnp.where(condition, 1.0, 0.0).astype(BF16)


def kept_column(c):
    return (c % 2) * HALF + c // 2


def to_kept():
    row, col = iota((LANES, LANES), 0), iota((LANES, LANES), 1)
    return one_hot(row // B * B + kept_column(row % B) == col)


def from_kept_twice():
    row, col = iota((2 * LANES, LANES), 0) % LANES, iota((2 * LANES, LANES), 1)
    return one_hot(col // B * B + kept_column(col % B) == row)


def pair_to_kept():
    row, col = iota((2 * LANES, 2 * LANES), 0), iota((2 * LANES, 2 * LANES), 1)
    w, p, c = row // LANES, row // B % 2, row % B
    return one_hot(p * LANES + w * B + kept_column(c) == col)


def blocks_first(order_ref, base, count, slots):
    col, row = iota((8, 8 * slots), 1), iota((8, 8 * slots), 0)
    same = col // slots == row
    slot = col % slots
    parts = [
        jnp.where(same & (slot == order_ref[base + k]), 1.0, 0.0) for k in range(count)
    ]
    return jnp.concatenate(parts, axis=0).astype(BF16)


def slots_last(order_ref, slots):
    n = 8 * slots
    place = iota((1, n), 1) // 8
    slot = jnp.zeros((1, n), jnp.int32)
    for k in range(slots):
        slot = jnp.where(place == k, order_ref[k], slot)
    row, col = iota((n, n), 0), iota((n, n), 1)
    return one_hot((row // slots == col % 8) & (row % slots == slot))


def inside(rows, cols):
    lane = iota((HALF, LANES), 1)
    a = 2 * iota((HALF, LANES), 0) + lane // B
    kept = lane % B
    c = 2 * (kept % HALF) + kept // HALF
    return jnp.where((a.astype(F32) < rows) & (c.astype(F32) < cols), 1.0, 0.0)


def total_of(x):
    return jnp.sum(jnp.sum(x, axis=0, keepdims=True), axis=1, keepdims=True)


def wide(x):
    return jnp.broadcast_to(x, (1, LANES))


def split(x):
    high = x.astype(BF16)
    return high, (x - high.astype(F32)).astype(BF16)


def split_three(x):
    high, _ = split(x)
    rest = x - high.astype(F32)
    middle, low = split(rest)
    return high, middle, low


def call(kernel, name, out_shape, operands, kinds, scratch=(), out_kinds=None, cost=2.0):
    space = {"s": pltpu.SMEM, "v": pltpu.VMEM, "a": pl.ANY}
    out_kinds = out_kinds or "v" * len(out_shape)
    return pl.pallas_call(
        kernel,
        out_shape=out_shape,
        in_specs=[pl.BlockSpec(memory_space=space[k]) for k in kinds],
        out_specs=tuple(pl.BlockSpec(memory_space=space[k]) for k in out_kinds),
        scratch_shapes=list(scratch),
        compiler_params=pltpu.CompilerParams(vmem_limit_bytes=VMEM_LIMIT),
        cost_estimate=pl.CostEstimate(flops=0, bytes_accessed=int(cost * 3.0e6), transcendentals=0),
        name=name,
    )(*operands)


def sort_slots(core, offset_ref, order_ref, place_ref, seen):
    slots = order_ref.shape[0]
    nodes = seen.shape[0]
    cap = slots // nodes
    for o in range(nodes):
        seen[o] = 0
    for j in range(slots):
        o = offset_ref[j]
        rank = seen[o]
        seen[o] = rank + 1
        place = o * cap + rank + core * (slots // 2)
        place = jnp.where(place >= slots, place - slots, place)
        order_ref[place] = j
        place_ref[j] = place


def arrange(order_ref, base, chan_ref, raw, wait, outs):
    chans, slots = raw.shape[1:3]
    cap = outs[0].shape[1]
    count = cap * len(outs)
    first = blocks_first(order_ref, base, count, slots)
    second = pair_to_kept()
    low = iota((1, 2 * LANES), 1) % LANES < B
    blank = jnp.zeros((slots, LANES), BF16)
    for t in range(2):
        for g in range(4):
            used = [w for w in (2 * g, 2 * g + 1) if w < chans]
            for w in used:
                wait(t, w)
            chunks = []
            for c in range(4):
                rows = []
                for i in range(8 * c, 8 * c + 8):
                    parts = [raw[t, w, :, i * LANES : (i + 1) * LANES] for w in used]
                    rows.append(jnp.concatenate(parts + [blank] * (2 - len(used)), axis=1))
                x = jnp.concatenate(rows, axis=0)
                x = jnp.dot(first, x, preferred_element_type=F32).astype(BF16)
                chunks.append(jnp.dot(x, second, preferred_element_type=F32))
            for k in range(count):
                x = jnp.concatenate([chunk[8 * k : 8 * k + 8] for chunk in chunks], axis=0)
                if t == 0:
                    slot = order_ref[base + k]
                    kept = [chan_ref[w, slot].astype(F32) for w in used]
                    x = x * jnp.where(low, kept[0], kept[-1])
                x = x.astype(BF16)
                for p in range(2):
                    outs[k // cap][t, k % cap, p * HALF : (p + 1) * HALF, g * LANES : (g + 1) * LANES] = x[
                        :, p * LANES : (p + 1) * LANES
                    ]


def fetcher(left_ref, right_ref, raw, sems):
    def copy(t, w):
        return pltpu.make_async_copy((left_ref, right_ref)[t].at[w], raw.at[t, w], sems.at[t, w])

    for t in range(2):
        for w in range(raw.shape[1]):
            copy(t, w).start()
    return lambda t, w: copy(t, w).wait()


def send_kernel(me_ref, offset_ref, chan_ref, left_ref, right_ref, order_ref, place_ref, near_ref, far_ref,
                raw, sems, seen):
    wait = fetcher(left_ref, right_ref, raw, sems)
    sort_slots(me_ref[1], offset_ref, order_ref, place_ref, seen)
    arrange(order_ref, order_ref.shape[0] // 2, chan_ref, raw, wait, (near_ref, far_ref))


def keep_kernel(order_ref, chan_ref, left_ref, right_ref, near_ref, far_ref, raw, sems):
    wait = fetcher(left_ref, right_ref, raw, sems)
    arrange(order_ref, 0, chan_ref, raw, wait, (near_ref, far_ref))


def ship_kernel(order_ref, ext_ref, start_ref, near_ref, far_ref, home_ref):
    slots = start_ref.shape[0]
    cap = slots // 4
    first = blocks_first(order_ref, 0, slots, slots)
    second = to_kept()
    chunks = []
    for c in range(4):
        rows = [start_ref[:, i * LANES : (i + 1) * LANES] for i in range(8 * c, 8 * c + 8)]
        x = jnp.dot(first, jnp.concatenate(rows, axis=0), preferred_element_type=F32).astype(BF16)
        chunks.append(jnp.dot(x, second, preferred_element_type=F32))
    halves = []
    for k in range(slots):
        slot = order_ref[k]
        x = jnp.concatenate([chunk[8 * k : 8 * k + 8] for chunk in chunks], axis=0)
        x = x * inside(ext_ref[0, slot].astype(F32), ext_ref[1, slot].astype(F32))
        home_ref[HALF * k : HALF * (k + 1), :] = x.astype(BF16)
        if k < 2 * cap:
            (near_ref, far_ref)[k // cap][HALF * (k % cap) : HALF * (k % cap + 1), :] = x.astype(BF16)
        if k % (2 * cap) == 0:
            halves.append(x * x)
        else:
            halves[-1] = halves[-1] + x * x
    squares = wide(total_of(halves[0]) + total_of(halves[1]))
    pieces = [v.astype(F32) for v in split_three(squares)]
    blank = jnp.zeros((2 * 16 - 2 * cap - 3, LANES), F32)
    for t, ref in enumerate((near_ref, far_ref)):
        lines = []
        for d in range(2):
            for k in range(cap):
                lines.append(jnp.full((1, LANES), ext_ref[d, order_ref[t * cap + k]].astype(F32)))
        ref[HALF * cap :, :] = jnp.concatenate(lines + pieces + [blank], axis=0).astype(BF16)


def note(ref):
    return ref[ref.shape[0] - 32 :, :].astype(F32)


def sums_kernel(near_ref, far_ref, out_ref):
    lines = []
    for ref in (near_ref, far_ref):
        n = note(ref)
        lines.append(n[16:17] + n[17:18] + n[18:19])
    out_ref[...] = jnp.concatenate(lines + [jnp.zeros((6, LANES), F32)], axis=0)


def block_diagonal(x):
    low = iota((HALF, LANES), 1) < B
    swapped = pltpu.roll(x, B, 1)
    zero = jnp.zeros_like(x)
    two = jnp.concatenate(
        [
            jnp.where(low, x, zero),
            jnp.where(low, swapped, zero),
            jnp.where(low, zero, swapped),
            jnp.where(low, zero, x),
        ],
        axis=0,
    )
    blank = jnp.zeros_like(two)
    return jnp.concatenate(
        [jnp.concatenate([two, blank], axis=1), jnp.concatenate([blank, two], axis=1)], axis=0
    )


def product(q_ref, keep_ref, got_ref, y_ref, inner_ref, rounded):
    count = q_ref.shape[0]
    span = 2 * LANES
    for s in range(count):
        high, low = split(block_diagonal(q_ref[s]))
        left = jnp.concatenate(
            [ref[0, s, :, g * span : (g + 1) * span] for ref in (keep_ref, got_ref) for g in range(2)], axis=0
        )
        inner = jnp.dot(left, high, preferred_element_type=F32)
        if not rounded:
            inner = inner + jnp.dot(left, low, preferred_element_type=F32)
        high, low = split(inner)
        for k in range(4):
            inner_ref[s, :B, k * span : (k + 1) * span] = high[k * B : (k + 1) * B]
            inner_ref[s, B:, k * span : (k + 1) * span] = low[k * B : (k + 1) * B]
    for s in range(count):
        right = jnp.concatenate([keep_ref[1, s], got_ref[1, s]], axis=1)
        both = lax.dot_general(inner_ref[s], right, (((1,), (1,)), ((), ())), preferred_element_type=F32)
        image = both[:B] + both[B:]
        y_ref[s] = jnp.concatenate([image[:HALF], image[HALF:]], axis=1)


def start_kernel(count, nodes, me_ref, ship_ref, sums_ref, more_ref, keep_ref, got_ref, q_ref, y_ref, scale_ref,
                 inner_ref):
    node, core = me_ref[0], me_ref[1]
    by_node = []
    for e in range(nodes):
        value = jnp.zeros((1, LANES), F32)
        for ref, c in ((sums_ref, core), (more_ref, 1 - core)):
            for t in range(2):
                source = lax.rem(node + 2 * nodes - 2 * c - t, nodes)
                value = value + jnp.where(source == e, ref[t : t + 1, :], 0.0)
        by_node.append(value)
    squares = (by_node[0] + by_node[1]) + (by_node[2] + by_node[3])
    scale = 1.0 / jnp.sqrt(squares / count + 1e-06)
    scale_ref[...] = jnp.broadcast_to(scale, scale_ref.shape)
    for s in range(q_ref.shape[0]):
        q_ref[s] = ship_ref[HALF * s : HALF * (s + 1), :].astype(F32) * scale
    product(q_ref, keep_ref, got_ref, y_ref, inner_ref, True)


def orthogonal(ship_ref, own_ref, other_ref, basis, q_ref):
    n = note(ship_ref)
    cap = q_ref.shape[0]
    for s in range(cap):
        q_ref[s] = (own_ref[s] + other_ref[s]) * inside(n[s : s + 1], n[cap + s : cap + s + 1])
    image = q_ref[...].reshape(cap * HALF, LANES)
    rows = []
    rest = image
    for ref in basis:
        q = ref[...].reshape(cap * HALF, LANES)
        length = total_of(q * q)
        along = total_of(q * image)
        row = wide(jnp.where(length > 0, along / jnp.where(length > 0, length, 1.0), 0.0))
        rest = rest - row * q
        rows.append(row)
    q_ref[...] = rest.reshape(q_ref.shape)
    return rows


def step_kernel(count, *refs):
    ship_ref, own_ref, other_ref = refs[:3]
    basis = refs[3 : 3 + count]
    keep_ref, got_ref, q_ref, y_ref, along_ref, inner_ref = refs[3 + count :]
    rows = orthogonal(ship_ref, own_ref, other_ref, basis, q_ref)
    along_ref[...] = jnp.concatenate(rows + [jnp.zeros((8 - count, LANES), F32)], axis=0)
    product(q_ref, keep_ref, got_ref, y_ref, inner_ref, False)


def table_kernel(*refs):
    out_refs, table_ref = refs[16:18], refs[18]
    rows = []
    for t in range(2):
        ship_ref, own_ref, other_ref, q0, q1, q2, c1, c2 = refs[8 * t : 8 * t + 8]
        last = orthogonal(ship_ref, own_ref, other_ref, (q0, q1, q2), out_refs[t])
        vectors = [ref[...].reshape(-1, LANES) for ref in (q0, q1, q2, out_refs[t])]
        for i in range(4):
            for j in range(i, 4):
                rows.append(wide(total_of(vectors[i] * vectors[j])))
        rows += [c1[0:1], c2[0:1], c2[1:2]] + last
    table_ref[...] = jnp.concatenate(rows, axis=0)


def pack_kernel(me_ref, table_ref, other_ref, *refs):
    core = me_ref[1]
    mine, other = table_ref[...], other_ref[...]
    tables = jnp.concatenate(
        [jnp.where(core == 0, mine, other), jnp.where(core == 0, other, mine)], axis=0
    )
    pieces = split_three(tables)
    for t in range(2):
        out_ref = refs[6 + t]
        at = 0
        for ref in refs[3 * t : 3 * t + 3]:
            rows = ref.shape[0] * HALF
            out_ref[at : at + rows, :] = ref[...].reshape(rows, LANES).astype(BF16)
            at += rows
        for piece in pieces:
            out_ref[at : at + piece.shape[0], :] = piece
            at += piece.shape[0]


def combine(count, take):
    gram = {}
    row = 0
    for i in range(4):
        for j in range(i, 4):
            gram[i, j] = gram[j, i] = take(row)
            row += 1
    one = jnp.ones_like(gram[0, 0])
    images = [
        [take(10), one, None, None],
        [take(11), take(12), one, None],
        [take(13), take(14), take(15), one],
    ]

    def mean(u, v):
        acc = None
        for i in range(4):
            for j in range(4):
                if u[i] is not None and v[j] is not None:
                    term = u[i] * v[j] * gram[i, j]
                    acc = term if acc is None else acc + term
        return jnp.sum(acc, axis=0, keepdims=True) / count

    basis = [[one, None, None, None]]
    projections = {}
    for k in range(ITERS):
        image = [None] * 4
        for z, parts in zip(basis[k], images):
            for m, v in enumerate(parts):
                if z is not None and v is not None:
                    image[m] = z * v if image[m] is None else image[m] + z * v
        rest = list(image)
        for i in range(k + 1):
            p = mean(basis[i], image)
            projections[i, k] = p
            for m, v in enumerate(basis[i]):
                if v is not None:
                    rest[m] = rest[m] - p * v
        if k + 1 < ITERS:
            scale = 1.0 / jnp.sqrt(mean(rest, rest) + 1e-06)
            basis.append([None if v is None else v * scale for v in rest])
    return projections, rest


def finish_kernel(count, nodes, me_ref, order_ref, scale_ref, home_ref, near_ref, far_ref, near_more_ref,
                  far_more_ref, out_ref, proj_ref, tables):
    node, core = me_ref[0], me_ref[1]
    slots = out_ref.shape[0]
    rows = home_ref.shape[0] // 4
    size = 4 * 16
    sources = []
    for k, ref in enumerate((near_ref, far_ref, near_more_ref, far_more_ref)):
        c = core if k < 2 else 1 - core
        hop = 2 * c + k % 2
        host = lax.rem(node + hop, nodes)
        pieces = [ref[3 * rows + d * size : 3 * rows + (d + 1) * size, :].astype(F32) for d in range(3)]
        tables[pl.ds(pl.multiple_of(host * size, size), size), :] = pieces[0] + pieces[1] + pieces[2]
        sources.append((ref, host * 4 + hop))
    sets = 4 * nodes
    projections, rest = combine(count, lambda k: tables[pl.ds(k, sets, stride=16), :])
    lines = []
    for i in range(ITERS):
        line = jnp.zeros((1, LANES), F32)
        for k in range(i, ITERS):
            line = jnp.where(iota((1, LANES), 1) == k, projections[i, k], line)
        lines.append(line)
    proj_ref[...] = jnp.concatenate(lines + [jnp.zeros((8 - ITERS, LANES), F32)], axis=0)
    scale = scale_ref[0:1, :]
    blocks = []
    for k, (ref, index) in enumerate(sources):
        mine = iota((sets, LANES), 0) == index
        coeff = [jnp.sum(jnp.where(mine, v, 0.0), axis=0, keepdims=True) for v in rest]
        x = coeff[0] * (home_ref[rows * k : rows * (k + 1), :].astype(F32) * scale)
        for d in range(3):
            x = x + coeff[d + 1] * ref[rows * d : rows * (d + 1), :].astype(F32)
        blocks.append(x)
    first = slots_last(order_ref, slots)
    second = from_kept_twice()
    per = rows // HALF
    for c in range(4):
        x = jnp.concatenate(
            [blocks[k // per][HALF * (k % per) + 8 * c : HALF * (k % per) + 8 * c + 8] for k in range(slots)],
            axis=0,
        )
        x = jnp.dot(first, jnp.concatenate(split(x), axis=1), preferred_element_type=F32).astype(BF16)
        x = jnp.dot(x, second, preferred_element_type=F32)
        for i in range(8):
            out_ref[:, (8 * c + i) * LANES : (8 * c + i + 1) * LANES] = x[i * slots : (i + 1) * slots]


def paired(start_vector, extents, offsets, env_left, env_right, channel_mask):
    nodes = lax.axis_size("sector")
    ops = lax.axis_size("op")
    node = lax.axis_index("sector")
    core = lax.axis_index("op") % 2
    slots = start_vector.shape[0]
    chans = env_left.shape[1]
    cap = slots // nodes
    count = float(slots * nodes * B * B)
    me = jnp.stack([node, core]).astype(jnp.int32)
    swap_core = [(i, i ^ 1) for i in range(ops)]
    swap_x = [(i, i ^ 2) for i in range(ops)]
    left = jnp.transpose(env_left, (1, 0, 2))
    right = jnp.transpose(env_right, (1, 0, 2))
    chan = jnp.transpose(channel_mask)
    ext = jnp.transpose(extents)

    def route(t, back):
        pairs = []
        for h in range(nodes):
            for q in range(ops):
                to = (h + 2 * (q % 2) + t) % nodes
                a, b = h * ops + q, to * ops + q
                pairs.append((b, a) if back else (a, b))
        return pairs

    def across(x):
        return lax.ppermute(x, "op", swap_core)

    def shape(dims, dtype=F32):
        return jax.ShapeDtypeStruct(dims, dtype)

    environment = shape((2, cap, B, WIDE), BF16)
    vector = shape((cap, HALF, LANES))
    tile = shape((8, LANES))
    raw = [pltpu.VMEM((2, chans, slots, B * B), BF16), pltpu.SemaphoreType.DMA((2, chans))]
    inner = [pltpu.VMEM((cap, LANES, 2 * WIDE), BF16)]

    order, _, *send = call(
        send_kernel, "send", (shape((slots,), jnp.int32), shape((slots,), jnp.int32), environment, environment),
        (me, offsets, chan, left, right), "sssaa", raw + [pltpu.SMEM((nodes,), jnp.int32)], "ssvv", 3.0)
    got = [across(x) for x in send]
    payload = shape((cap * HALF + 32, LANES), BF16)
    *ships, home = call(
        ship_kernel, "ship", (payload, payload, shape((slots * HALF, LANES), BF16)),
        (order, ext, start_vector), "ssv", cost=1.0)
    ships = [lax.ppermute(x, ("sector", "op"), route(t, False)) for t, x in enumerate(ships)]
    keep = call(
        keep_kernel, "keep", (environment, environment), (order, chan, left, right), "ssaa", raw, cost=3.0)
    (sums,) = call(sums_kernel, "sums", (tile,), ships, "vv", cost=0.3)
    more = across(sums)

    def start(*refs):
        start_kernel(count, nodes, *refs)

    def step(k):
        return lambda *refs: step_kernel(k, *refs)

    basis = [[], []]
    along = [[], []]
    images = [None, None]
    for t in range(2):
        q, y, scale = call(
            start, "first", (vector, vector, tile), (me, ships[t], sums, more, keep[t], got[t]), "svvvvv", inner)
        basis[t].append(q)
        images[t] = (y, lax.ppermute(y, "op", swap_x))
    for k in range(1, ITERS):
        for t in range(2):
            q, y, a = call(
                step(k), ("second", "third")[k - 1], (vector, vector, tile),
                (ships[t], *images[t], *basis[t], keep[t], got[t]), "v" * (5 + k), inner)
            basis[t].append(q)
            along[t].append(a)
            images[t] = (y, lax.ppermute(y, "op", swap_x))

    operands = []
    for t in range(2):
        operands += [ships[t], *images[t], *basis[t], *along[t]]
    *last, table = call(
        table_kernel, "table", (vector, vector, shape((32, LANES))), operands, "v" * 16, cost=1.0)
    other_table = across(table)
    vectors = []
    for t in range(2):
        vectors += [basis[t][1], basis[t][2], last[t]]
    parcel = shape((3 * cap * HALF + 3 * 64, LANES), BF16)
    parcels = call(
        pack_kernel, "pack", (parcel, parcel), (me, table, other_table, *vectors), "s" + "v" * 8, cost=0.7)
    parcels = [lax.ppermute(x, ("sector", "op"), route(t, True)) for t, x in enumerate(parcels)]
    parcels += [across(x) for x in parcels]

    def finish(*refs):
        finish_kernel(count, nodes, *refs)

    residual, proj = call(
        finish, "finish", (shape((slots, B * B)), tile), (me, order, scale, home, *parcels), "ssvvvvvv",
        [pltpu.VMEM((4 * nodes * 16, LANES), F32)])
    return residual, proj[:ITERS, :ITERS]


def pack_rows(data, index, nodes, cap):
    slots = data.shape[0]
    hit = jnp.arange(nodes * cap, dtype=jnp.int32)[:, None] == index[None, :]
    source = jnp.sum(jnp.where(hit, jnp.arange(slots, dtype=jnp.int32)[None, :], 0), axis=1)
    filled = jnp.any(hit, axis=1)
    rows = jnp.take(data, source, axis=0)
    rows = jnp.where(filled[:, None], rows, jnp.zeros_like(rows))
    return rows.reshape(nodes, cap, data.shape[1])


def unpack_rows(arrived, index):
    flat = arrived.reshape(arrived.shape[0] * arrived.shape[1], arrived.shape[2])
    return jnp.take(flat, index, axis=0)


def general(start_vector, extents, offsets, env_left, env_right, channel_mask):
    nodes = lax.axis_size("sector")
    here_index = lax.axis_index("sector")
    slots = start_vector.shape[0]
    cap = max(1, slots // nodes)
    chans = env_left.shape[1]
    count = float(slots * nodes * B * B)
    slot_ids = jnp.arange(slots, dtype=jnp.int32)
    same = offsets[:, None] == offsets[None, :]
    earlier = slot_ids[None, :] < slot_ids[:, None]
    rank = jnp.sum((same & earlier).astype(jnp.int32), axis=1)
    send_index = (here_index + offsets) % nodes * cap + rank
    recv_index = (here_index - offsets) % nodes * cap + rank
    position = jnp.arange(B * B, dtype=jnp.int32)
    inside = ((position // B)[None, :] < extents[:, 0:1]) & (
        (position % B)[None, :] < extents[:, 1:2]
    )
    mask = inside.astype(jnp.float32)
    left = env_left.reshape(slots, chans, B, B)
    right_wide = env_right.reshape(slots, chans, B, B).astype(jnp.float32)
    chan = channel_mask.astype(jnp.float32)

    def squares(vector):
        return lax.psum(jnp.sum(vector * vector), "sector") / count

    def correlation_table(basis, image):
        local = [jnp.sum(vector * image) for vector in basis]
        local = local + [jnp.zeros((), jnp.float32)] * (ITERS - len(basis))
        return lax.psum(jnp.stack(local), "sector") / count

    masked = mask * start_vector.astype(jnp.float32)
    basis = [masked / jnp.sqrt(squares(masked) + 1e-06)]
    projections = jnp.zeros((ITERS, ITERS), jnp.float32)
    residual = masked
    for step in range(ITERS):
        moving = pack_rows(basis[step].astype(jnp.bfloat16), send_index, nodes, cap)
        arrived = lax.all_to_all(moving, "sector", split_axis=0, concat_axis=0, tiled=True)
        blocks = unpack_rows(arrived, recv_index).reshape(slots, B, B)
        inner = jnp.einsum("swab,sbc->swac", left, blocks, preferred_element_type=jnp.float32)
        inner = inner * chan[:, :, None, None]
        partial_image = jnp.einsum(
            "swac,swdc->sad", inner, right_wide, precision=lax.Precision.HIGHEST
        )
        total = lax.psum(partial_image.reshape(slots, B * B), "op")
        going = pack_rows(total, recv_index, nodes, cap)
        returned = lax.all_to_all(going, "sector", split_axis=0, concat_axis=0, tiled=True)
        apply_image = unpack_rows(returned, send_index)
        image = apply_image * mask
        coeffs = correlation_table(basis, image)
        residual = image
        for index in range(step + 1):
            projections = projections.at[index, step].set(coeffs[index])
            residual = residual - coeffs[index] * basis[index]
        if step + 1 < ITERS:
            basis.append(residual / jnp.sqrt(squares(residual) + 1e-06))
    return (residual, projections)


def solution(mesh):
    def on_device(start_vector, extents, offsets, env_left, env_right, channel_mask):
        nodes, ops = mesh.shape["sector"], mesh.shape["op"]
        slots, chans = env_left.shape[:2]
        fits = nodes == 4 and ops == 4 and slots == 8 * nodes and chans <= 8
        body = paired if fits else general
        return body(start_vector, extents, offsets, env_left, env_right, channel_mask)

    return jax.shard_map(
        on_device,
        mesh=mesh,
        in_specs=(
            P(("groups", "sector"), None),
            P(("groups", "sector"), None),
            P("groups"),
            P(("groups", "sector"), "op", None),
            P(("groups", "sector"), "op", None),
            P(("groups", "sector"), "op"),
        ),
        out_specs=(P(("groups", "sector"), None), P("groups", None)),
        check_vma=False,
    )
```

```python
import jax
import jax.numpy as jnp
from jax import lax
from jax.experimental import pallas as pl
from jax.experimental.pallas import tpu as pltpu
from jax.sharding import PartitionSpec as P

B = 64
ITERS = 3
HALF = 32
LANES = 128
WIDE = 4 * LANES
F32 = jnp.float32
BF16 = jnp.bfloat16
VMEM_LIMIT = 24 * 1024 * 1024
ROOMY = 32 * 1024 * 1024
ARRANGE = 32 * 1024 * 1024


def position():
    return lax.axis_index("sector"), lax.axis_index("op") % 2


def iota(shape, dim):
    return lax.broadcasted_iota(jnp.int32, shape, dim)


def one_hot(condition):
    return jnp.where(condition, 1.0, 0.0).astype(BF16)


def kept_column(c):
    return (c % 2) * HALF + c // 2


def to_kept():
    row, col = iota((LANES, LANES), 0), iota((LANES, LANES), 1)
    return one_hot(row // B * B + kept_column(row % B) == col)


def from_kept_twice():
    row, col = iota((2 * LANES, LANES), 0) % LANES, iota((2 * LANES, LANES), 1)
    return one_hot(col // B * B + kept_column(col % B) == row)


def pair_to_kept():
    row, col = iota((2 * LANES, 2 * LANES), 0), iota((2 * LANES, 2 * LANES), 1)
    w, p, c = row // LANES, row // B % 2, row % B
    return one_hot(p * LANES + w * B + kept_column(c) == col)


def blocks_first(order_ref, base, count, slots):
    col, row = iota((8, 8 * slots), 1), iota((8, 8 * slots), 0)
    same = col // slots == row
    slot = col % slots
    parts = [
        jnp.where(same & (slot == order_ref[base + k]), 1.0, 0.0) for k in range(count)
    ]
    return jnp.concatenate(parts, axis=0).astype(BF16)


def slots_last(order_ref, slots):
    n = 8 * slots
    place = iota((1, n), 1) // 8
    slot = jnp.zeros((1, n), jnp.int32)
    for k in range(slots):
        slot = jnp.where(place == k, order_ref[k], slot)
    row, col = iota((n, n), 0), iota((n, n), 1)
    return one_hot((row // slots == col % 8) & (row % slots == slot))


def inside(rows, cols):
    lane = iota((HALF, LANES), 1)
    a = 2 * iota((HALF, LANES), 0) + lane // B
    kept = lane % B
    c = 2 * (kept % HALF) + kept // HALF
    return jnp.where((a.astype(F32) < rows) & (c.astype(F32) < cols), 1.0, 0.0)


def total_of(x):
    return jnp.sum(jnp.sum(x, axis=0, keepdims=True), axis=1, keepdims=True)


def wide(x):
    return jnp.broadcast_to(x, (1, LANES))


def split(x):
    high = x.astype(BF16)
    return high, (x - high.astype(F32)).astype(BF16)


def split_three(x):
    high, _ = split(x)
    rest = x - high.astype(F32)
    middle, low = split(rest)
    return high, middle, low


def call(kernel, name, out_shape, operands, kinds, scratch=(), out_kinds=None, cost=2.0, limit=VMEM_LIMIT,
         compute=False):
    space = {"s": pltpu.SMEM, "v": pltpu.VMEM, "h": pltpu.HBM, "a": pl.ANY}
    out_kinds = out_kinds or "v" * len(out_shape)
    return pl.pallas_call(
        kernel,
        out_shape=out_shape,
        in_specs=[pl.BlockSpec(memory_space=space[k]) for k in kinds],
        out_specs=tuple(pl.BlockSpec(memory_space=space[k]) for k in out_kinds),
        scratch_shapes=list(scratch),
        compiler_params=pltpu.CompilerParams(vmem_limit_bytes=limit),
        cost_estimate=pl.CostEstimate(
            flops=int(cost * 1.0e9) if compute else 0,
            bytes_accessed=1024 if compute else int(cost * 3.0e6),
            transcendentals=0,
        ),
        name=name,
    )(*operands)


def sort_slots(core, meta_ref, order_ref, seen):
    slots = order_ref.shape[0]
    nodes = seen.shape[0]
    cap = slots // nodes
    for o in range(nodes):
        seen[o] = 0
    for j in range(slots):
        o = meta_ref[0, j]
        rank = seen[o]
        seen[o] = rank + 1
        place = o * cap + rank + core * (slots // 2)
        order_ref[jnp.where(place >= slots, place - slots, place)] = j


def arrange_kernel(masked, order_ref, meta_ref, env_ref, _, *outs):
    chans, slots = env_ref.shape[:2]
    cap = outs[0].shape[0]
    first = blocks_first(order_ref, 0, slots, slots)
    second = pair_to_kept()
    low = iota((1, 2 * LANES), 1) % LANES < B
    blank = jnp.zeros((slots, LANES), BF16)
    for g in range(4):
        used = [w for w in (2 * g, 2 * g + 1) if w < chans]
        chunks = []
        for c in range(4):
            rows = []
            for i in range(8 * c, 8 * c + 8):
                parts = [env_ref[w, :, i * LANES : (i + 1) * LANES] for w in used]
                rows.append(jnp.concatenate(parts + [blank] * (2 - len(used)), axis=1))
            x = jnp.concatenate(rows, axis=0)
            x = jnp.dot(first, x, preferred_element_type=F32).astype(BF16)
            chunks.append(jnp.dot(x, second, preferred_element_type=F32))
        for k in range(slots):
            x = jnp.concatenate([chunk[8 * k : 8 * k + 8] for chunk in chunks], axis=0)
            if masked:
                slot = order_ref[k]
                kept = [meta_ref[3 + w, slot].astype(F32) for w in used]
                x = x * jnp.where(low, kept[0], kept[-1])
            x = x.astype(BF16)
            for p in range(2):
                outs[k // cap][k % cap, p * HALF : (p + 1) * HALF, g * LANES : (g + 1) * LANES] = x[
                    :, p * LANES : (p + 1) * LANES
                ]


def ship_kernel(meta_ref, start_ref, order_ref, near_ref, far_ref, home_ref, seen):
    sort_slots(position()[1], meta_ref, order_ref, seen)
    slots = start_ref.shape[0]
    cap = slots // 4
    first = blocks_first(order_ref, 0, slots, slots)
    second = to_kept()
    chunks = []
    for c in range(4):
        rows = [start_ref[:, i * LANES : (i + 1) * LANES] for i in range(8 * c, 8 * c + 8)]
        x = jnp.dot(first, jnp.concatenate(rows, axis=0), preferred_element_type=F32).astype(BF16)
        chunks.append(jnp.dot(x, second, preferred_element_type=F32))
    halves = []
    for k in range(slots):
        slot = order_ref[k]
        x = jnp.concatenate([chunk[8 * k : 8 * k + 8] for chunk in chunks], axis=0)
        x = x * inside(meta_ref[1, slot].astype(F32), meta_ref[2, slot].astype(F32))
        home_ref[HALF * k : HALF * (k + 1), :] = x.astype(BF16)
        if k < 2 * cap:
            (near_ref, far_ref)[k // cap][HALF * (k % cap) : HALF * (k % cap + 1), :] = x.astype(BF16)
        if k % (2 * cap) == 0:
            halves.append(x * x)
        else:
            halves[-1] = halves[-1] + x * x
    squares = wide(total_of(halves[0]) + total_of(halves[1]))
    pieces = [v.astype(F32) for v in split_three(squares)]
    blank = jnp.zeros((2 * 16 - 2 * cap - 3, LANES), F32)
    for t, ref in enumerate((near_ref, far_ref)):
        lines = []
        for d in range(2):
            for k in range(cap):
                lines.append(jnp.full((1, LANES), meta_ref[1 + d, order_ref[t * cap + k]].astype(F32)))
        ref[HALF * cap :, :] = jnp.concatenate(lines + pieces + [blank], axis=0).astype(BF16)


def note(ref):
    return ref[ref.shape[0] - 32 :, :].astype(F32)


def sums_kernel(near_ref, far_ref, _, out_ref):
    lines = []
    for ref in (near_ref, far_ref):
        n = note(ref)
        lines.append(n[16:17] + n[17:18] + n[18:19])
    out_ref[...] = jnp.concatenate(lines + [jnp.zeros((6, LANES), F32)], axis=0)


def block_diagonal(x):
    low = iota((HALF, LANES), 1) < B
    swapped = pltpu.roll(x, B, 1)
    zero = jnp.zeros_like(x)
    two = jnp.concatenate(
        [
            jnp.where(low, x, zero),
            jnp.where(low, swapped, zero),
            jnp.where(low, zero, swapped),
            jnp.where(low, zero, x),
        ],
        axis=0,
    )
    blank = jnp.zeros_like(two)
    return jnp.concatenate(
        [jnp.concatenate([two, blank], axis=1), jnp.concatenate([blank, two], axis=1)], axis=0
    )


def product(q_ref, envs, y_ref, inner_ref, rounded):
    count = q_ref.shape[0]
    span = 2 * LANES
    keep_left, keep_right, got_left, got_right = envs
    for s in range(count):
        high, low = split(block_diagonal(q_ref[s]))
        left = jnp.concatenate(
            [ref[s, :, g * span : (g + 1) * span] for ref in (keep_left, got_left) for g in range(2)], axis=0
        )
        inner = jnp.dot(left, high, preferred_element_type=F32)
        if not rounded:
            inner = inner + jnp.dot(left, low, preferred_element_type=F32)
        high, low = split(inner)
        for k in range(4):
            inner_ref[s, :B, k * span : (k + 1) * span] = high[k * B : (k + 1) * B]
            inner_ref[s, B:, k * span : (k + 1) * span] = low[k * B : (k + 1) * B]
    for s in range(count):
        right = jnp.concatenate([keep_right[s], got_right[s]], axis=1)
        both = lax.dot_general(inner_ref[s], right, (((1,), (1,)), ((), ())), preferred_element_type=F32)
        image = both[:B] + both[B:]
        y_ref[s] = jnp.concatenate([image[:HALF], image[HALF:]], axis=1)


def start_kernel(count, nodes, ship_ref, sums_ref, more_ref, *refs):
    envs, (q_ref, y_ref, scale_ref, inner_ref) = refs[:4], refs[4:]
    node, core = position()
    by_node = []
    for e in range(nodes):
        value = jnp.zeros((1, LANES), F32)
        for ref, c in ((sums_ref, core), (more_ref, 1 - core)):
            for t in range(2):
                source = lax.rem(node + 2 * nodes - 2 * c - t, nodes)
                value = value + jnp.where(source == e, ref[t : t + 1, :], 0.0)
        by_node.append(value)
    squares = (by_node[0] + by_node[1]) + (by_node[2] + by_node[3])
    scale = 1.0 / jnp.sqrt(squares / count + 1e-06)
    scale_ref[...] = jnp.broadcast_to(scale, scale_ref.shape)
    for s in range(q_ref.shape[0]):
        q_ref[s] = ship_ref[HALF * s : HALF * (s + 1), :].astype(F32) * scale
    product(q_ref, envs, y_ref, inner_ref, True)


def orthogonal(ship_ref, own_ref, other_ref, basis, q_ref):
    n = note(ship_ref)
    cap = q_ref.shape[0]
    for s in range(cap):
        q_ref[s] = (own_ref[s] + other_ref[s]) * inside(n[s : s + 1], n[cap + s : cap + s + 1])
    image = q_ref[...].reshape(cap * HALF, LANES)
    rows = []
    rest = image
    for ref in basis:
        q = ref[...].reshape(cap * HALF, LANES)
        length = total_of(q * q)
        along = total_of(q * image)
        row = wide(jnp.where(length > 0, along / jnp.where(length > 0, length, 1.0), 0.0))
        rest = rest - row * q
        rows.append(row)
    q_ref[...] = rest.reshape(q_ref.shape)
    return rows


def step_kernel(count, *refs):
    ship_ref, own_ref, other_ref = refs[:3]
    basis = refs[3 : 3 + count]
    envs = refs[3 + count : 7 + count]
    q_ref, y_ref, along_ref, *parcel_ref, inner_ref = refs[7 + count :]
    rows = orthogonal(ship_ref, own_ref, other_ref, basis, q_ref)
    along_ref[...] = jnp.concatenate(rows + [jnp.zeros((8 - count, LANES), F32)], axis=0)
    for ref in parcel_ref:
        vectors = [r[...].reshape(-1, LANES) for r in (*basis[1:], q_ref)]
        ref[...] = jnp.concatenate(vectors, axis=0).astype(BF16)
    product(q_ref, envs, y_ref, inner_ref, False)


def line_of(values):
    lane = iota((1, LANES), 1)
    line = jnp.zeros((1, LANES), F32)
    for k, value in enumerate(values):
        line = jnp.where(lane == k, value, line)
    return line


def table_kernel(*refs):
    out_refs, table_ref = refs[16:18], refs[18]
    lines = []
    for t in range(2):
        ship_ref, own_ref, other_ref, q0, q1, q2, c1, c2 = refs[8 * t : 8 * t + 8]
        last = orthogonal(ship_ref, own_ref, other_ref, (q0, q1, q2), out_refs[t])
        vectors = [ref[...].reshape(-1, LANES) for ref in (q0, q1, q2, out_refs[t])]
        values = [total_of(vectors[i] * vectors[j]) for i in range(4) for j in range(i, 4)]
        lines.append(line_of(values + [c1[0:1], c2[0:1], c2[1:2]] + last))
    table_ref[...] = jnp.concatenate(lines + [jnp.zeros((6, LANES), F32)], axis=0)


def pack_kernel(table_ref, other_ref, *refs):
    core = position()[1]
    mine, other = table_ref[0:2, :], other_ref[0:2, :]
    lines = jnp.concatenate([jnp.where(core == 0, mine, other), jnp.where(core == 0, other, mine)], axis=0)
    pieces = [v.astype(F32) for v in split_three(lines)]
    tail = jnp.concatenate(pieces + [jnp.zeros((4, LANES), F32)], axis=0).astype(BF16)
    for ref, out_ref in zip(refs[:2], refs[2:]):
        rows = ref.shape[0] * HALF
        out_ref[:rows, :] = ref[...].reshape(rows, LANES).astype(BF16)
        out_ref[rows:, :] = tail


def combine(count, take):
    gram = {}
    row = 0
    for i in range(4):
        for j in range(i, 4):
            gram[i, j] = gram[j, i] = take(row)
            row += 1
    one = jnp.ones_like(gram[0, 0])
    images = [
        [take(10), one, None, None],
        [take(11), take(12), one, None],
        [take(13), take(14), take(15), one],
    ]

    def mean(u, v):
        acc = None
        for i in range(4):
            for j in range(4):
                if u[i] is not None and v[j] is not None:
                    term = u[i] * v[j] * gram[i, j]
                    acc = term if acc is None else acc + term
        return jnp.sum(acc, axis=0, keepdims=True) / count

    basis = [[one, None, None, None]]
    projections = {}
    for k in range(ITERS):
        image = [None] * 4
        for z, parts in zip(basis[k], images):
            for m, v in enumerate(parts):
                if z is not None and v is not None:
                    image[m] = z * v if image[m] is None else image[m] + z * v
        rest = list(image)
        for i in range(k + 1):
            p = mean(basis[i], image)
            projections[i, k] = p
            for m, v in enumerate(basis[i]):
                if v is not None:
                    rest[m] = rest[m] - p * v
        if k + 1 < ITERS:
            scale = 1.0 / jnp.sqrt(mean(rest, rest) + 1e-06)
            basis.append([None if v is None else v * scale for v in rest])
    return projections, rest


def finish_kernel(count, nodes, order_ref, scale_ref, home_ref, *refs):
    early, late, (out_ref, proj_ref) = refs[:4], refs[4:8], refs[8:]
    node, core = position()
    slots = out_ref.shape[0]
    rows = home_ref.shape[0] // 4
    sources = []
    lines = [jnp.zeros((4, LANES), F32) for _ in range(nodes)]
    for k, ref in enumerate(late):
        hop = 2 * (core if k < 2 else 1 - core) + k % 2
        host = lax.rem(node + hop, nodes)
        tail = ref[rows:, :].astype(F32)
        four = tail[0:4] + tail[4:8] + tail[8:12]
        lines = [jnp.where(host == e, four, v) for e, v in enumerate(lines)]
        sources.append((early[k], ref, host * 4 + hop))
    table = jnp.concatenate(lines, axis=0)
    sets = 4 * nodes
    projections, rest = combine(
        count, lambda k: jnp.broadcast_to(table[:, k : k + 1], (sets, LANES)))
    lines = [line_of([projections.get((i, k), 0.0) for k in range(ITERS)]) for i in range(ITERS)]
    proj_ref[...] = jnp.concatenate(lines, axis=0)[:, :ITERS]
    scale = scale_ref[0:1, :]
    blocks = []
    for k, (two, one, index) in enumerate(sources):
        mine = iota((sets, LANES), 0) == index
        coeff = [jnp.sum(jnp.where(mine, v, 0.0), axis=0, keepdims=True) for v in rest]
        x = coeff[0] * (home_ref[rows * k : rows * (k + 1), :].astype(F32) * scale)
        x = x + coeff[1] * two[:rows, :].astype(F32) + coeff[2] * two[rows:, :].astype(F32)
        x = x + coeff[3] * one[:rows, :].astype(F32)
        blocks.append(x)
    first = slots_last(order_ref, slots)
    second = from_kept_twice()
    per = rows // HALF
    for c in range(4):
        x = jnp.concatenate(
            [blocks[k // per][HALF * (k % per) + 8 * c : HALF * (k % per) + 8 * c + 8] for k in range(slots)],
            axis=0,
        )
        x = jnp.dot(first, jnp.concatenate(split(x), axis=1), preferred_element_type=F32).astype(BF16)
        x = jnp.dot(x, second, preferred_element_type=F32)
        for i in range(8):
            out_ref[:, (8 * c + i) * LANES : (8 * c + i + 1) * LANES] = x[i * slots : (i + 1) * slots]


def paired(start_vector, extents, offsets, env_left, env_right, channel_mask):
    nodes = lax.axis_size("sector")
    ops = lax.axis_size("op")
    slots = start_vector.shape[0]
    cap = slots // nodes
    count = float(slots * nodes * B * B)
    swap_core = [(i, i ^ 1) for i in range(ops)]
    swap_x = [(i, i ^ 2) for i in range(ops)]
    left = jnp.transpose(env_left, (1, 0, 2))
    right = jnp.transpose(env_right, (1, 0, 2))
    meta = jnp.concatenate([offsets[None], jnp.transpose(extents), jnp.transpose(channel_mask)], axis=0)

    def route(t, back):
        pairs = []
        for h in range(nodes):
            for q in range(ops):
                to = (h + 2 * (q % 2) + t) % nodes
                a, b = h * ops + q, to * ops + q
                pairs.append((b, a) if back else (a, b))
        return pairs

    def across(x):
        return lax.ppermute(x, "op", swap_core)

    def shape(dims, dtype=F32):
        return jax.ShapeDtypeStruct(dims, dtype)

    environment = shape((cap, B, WIDE), BF16)
    vector = shape((cap, HALF, LANES))
    tile = shape((8, LANES))
    payload = shape((cap * HALF + 32, LANES), BF16)
    order, *ships, home = call(
        ship_kernel, "ship",
        (shape((slots,), jnp.int32), payload, payload, shape((slots * HALF, LANES), BF16)),
        (meta, start_vector), "sv", [pltpu.SMEM((nodes,), jnp.int32)], "svvv", 2.0, ROOMY, True)
    ships = [lax.ppermute(x, ("sector", "op"), route(t, False)) for t, x in enumerate(ships)]

    def arrange(masked, env, after):
        sets = call(
            lambda *refs: arrange_kernel(masked, *refs), "arrange", (environment,) * 4, (order, meta, env, after),
            "ssva", cost=3.0, limit=ARRANGE, compute=True)
        return sets[:2], [across(x) for x in sets[2:]]

    keep_left, got_left = arrange(True, left, order)
    (sums,) = call(sums_kernel, "sums", (tile,), (*ships, keep_left[0]), "vva", cost=0.3)
    keep_right, got_right = arrange(False, right, sums)
    envs = [(keep_left[t], keep_right[t], got_left[t], got_right[t]) for t in range(2)]
    more = across(sums)

    def start(*refs):
        start_kernel(count, nodes, *refs)

    def step(k):
        return lambda *refs: step_kernel(k, *refs)

    inner = [pltpu.VMEM((cap, LANES, 2 * WIDE), BF16)]
    basis = [[], []]
    along = [[], []]
    images = [None, None]
    early = []
    for t in range(2):
        q, y, scale = call(
            start, "first", (vector, vector, tile), (ships[t], sums, more, *envs[t]), "v" * 7, inner)
        basis[t].append(q)
        images[t] = (y, lax.ppermute(y, "op", swap_x))
    for k in range(1, ITERS):
        for t in range(2):
            outs = [vector, vector, tile]
            if k == ITERS - 1:
                outs.append(shape((2 * cap * HALF, LANES), BF16))
            q, y, a, *parcel = call(
                step(k), ("second", "third")[k - 1], tuple(outs),
                (ships[t], *images[t], *basis[t], *envs[t]), "v" * (7 + k), inner)
            basis[t].append(q)
            along[t].append(a)
            images[t] = (y, lax.ppermute(y, "op", swap_x))
            early += [lax.ppermute(x, ("sector", "op"), route(t, True)) for x in parcel]
    early += [across(x) for x in early]

    operands = []
    for t in range(2):
        operands += [ships[t], *images[t], *basis[t], *along[t]]
    *last, table = call(table_kernel, "table", (vector, vector, tile), operands, "v" * 16, cost=1.0)
    parcel = shape((cap * HALF + 16, LANES), BF16)
    late = call(
        pack_kernel, "pack", (parcel, parcel), (table, across(table), *last), "vvvv", cost=0.7)
    late = [lax.ppermute(x, ("sector", "op"), route(t, True)) for t, x in enumerate(late)]
    late += [across(x) for x in late]

    def finish(*refs):
        finish_kernel(count, nodes, *refs)

    return call(
        finish, "finish", (shape((slots, B * B)), shape((ITERS, ITERS))),
        (order, scale, home, *early, *late), "s" + "v" * 10)


def pack_rows(data, index, nodes, cap):
    slots = data.shape[0]
    hit = jnp.arange(nodes * cap, dtype=jnp.int32)[:, None] == index[None, :]
    source = jnp.sum(jnp.where(hit, jnp.arange(slots, dtype=jnp.int32)[None, :], 0), axis=1)
    filled = jnp.any(hit, axis=1)
    rows = jnp.take(data, source, axis=0)
    rows = jnp.where(filled[:, None], rows, jnp.zeros_like(rows))
    return rows.reshape(nodes, cap, data.shape[1])


def unpack_rows(arrived, index):
    flat = arrived.reshape(arrived.shape[0] * arrived.shape[1], arrived.shape[2])
    return jnp.take(flat, index, axis=0)


def general(start_vector, extents, offsets, env_left, env_right, channel_mask):
    nodes = lax.axis_size("sector")
    here_index = lax.axis_index("sector")
    slots = start_vector.shape[0]
    cap = max(1, slots // nodes)
    chans = env_left.shape[1]
    count = float(slots * nodes * B * B)
    slot_ids = jnp.arange(slots, dtype=jnp.int32)
    same = offsets[:, None] == offsets[None, :]
    earlier = slot_ids[None, :] < slot_ids[:, None]
    rank = jnp.sum((same & earlier).astype(jnp.int32), axis=1)
    send_index = (here_index + offsets) % nodes * cap + rank
    recv_index = (here_index - offsets) % nodes * cap + rank
    position = jnp.arange(B * B, dtype=jnp.int32)
    inside = ((position // B)[None, :] < extents[:, 0:1]) & (
        (position % B)[None, :] < extents[:, 1:2]
    )
    mask = inside.astype(jnp.float32)
    left = env_left.reshape(slots, chans, B, B)
    right_wide = env_right.reshape(slots, chans, B, B).astype(jnp.float32)
    chan = channel_mask.astype(jnp.float32)

    def squares(vector):
        return lax.psum(jnp.sum(vector * vector), "sector") / count

    def correlation_table(basis, image):
        local = [jnp.sum(vector * image) for vector in basis]
        local = local + [jnp.zeros((), jnp.float32)] * (ITERS - len(basis))
        return lax.psum(jnp.stack(local), "sector") / count

    masked = mask * start_vector.astype(jnp.float32)
    basis = [masked / jnp.sqrt(squares(masked) + 1e-06)]
    projections = jnp.zeros((ITERS, ITERS), jnp.float32)
    residual = masked
    for step in range(ITERS):
        moving = pack_rows(basis[step].astype(jnp.bfloat16), send_index, nodes, cap)
        arrived = lax.all_to_all(moving, "sector", split_axis=0, concat_axis=0, tiled=True)
        blocks = unpack_rows(arrived, recv_index).reshape(slots, B, B)
        inner = jnp.einsum("swab,sbc->swac", left, blocks, preferred_element_type=jnp.float32)
        inner = inner * chan[:, :, None, None]
        partial_image = jnp.einsum(
            "swac,swdc->sad", inner, right_wide, precision=lax.Precision.HIGHEST
        )
        total = lax.psum(partial_image.reshape(slots, B * B), "op")
        going = pack_rows(total, recv_index, nodes, cap)
        returned = lax.all_to_all(going, "sector", split_axis=0, concat_axis=0, tiled=True)
        apply_image = unpack_rows(returned, send_index)
        image = apply_image * mask
        coeffs = correlation_table(basis, image)
        residual = image
        for index in range(step + 1):
            projections = projections.at[index, step].set(coeffs[index])
            residual = residual - coeffs[index] * basis[index]
        if step + 1 < ITERS:
            basis.append(residual / jnp.sqrt(squares(residual) + 1e-06))
    return (residual, projections)


def solution(mesh):
    def on_device(start_vector, extents, offsets, env_left, env_right, channel_mask):
        nodes, ops = mesh.shape["sector"], mesh.shape["op"]
        slots, chans = env_left.shape[:2]
        fits = nodes == 4 and ops == 4 and slots == 8 * nodes and chans <= 8
        body = paired if fits else general
        return body(start_vector, extents, offsets, env_left, env_right, channel_mask)

    return jax.shard_map(
        on_device,
        mesh=mesh,
        in_specs=(
            P(("groups", "sector"), None),
            P(("groups", "sector"), None),
            P("groups"),
            P(("groups", "sector"), "op", None),
            P(("groups", "sector"), "op", None),
            P(("groups", "sector"), "op"),
        ),
        out_specs=(P(("groups", "sector"), None), P("groups", None)),
        check_vma=False,
    )
```

```python
import jax
import jax.numpy as jnp
from jax import lax
from jax.experimental import pallas as pl
from jax.experimental.pallas import tpu as pltpu
from jax.sharding import PartitionSpec as P

B = 64
ITERS = 3
HALF = 32
LANES = 128
WIDE = 4 * LANES
F32 = jnp.float32
BF16 = jnp.bfloat16
VMEM_LIMIT = 24 * 1024 * 1024
ROOMY = 32 * 1024 * 1024
ARRANGE = 32 * 1024 * 1024


def position():
    return lax.axis_index("sector"), lax.axis_index("op") % 2


def iota(shape, dim):
    return lax.broadcasted_iota(jnp.int32, shape, dim)


def one_hot(condition):
    return jnp.where(condition, 1.0, 0.0).astype(BF16)


def kept_column(c):
    return (c % 2) * HALF + c // 2


def to_kept():
    row, col = iota((LANES, LANES), 0), iota((LANES, LANES), 1)
    return one_hot(row // B * B + kept_column(row % B) == col)


def from_kept_twice():
    row, col = iota((2 * LANES, LANES), 0) % LANES, iota((2 * LANES, LANES), 1)
    return one_hot(col // B * B + kept_column(col % B) == row)


def pair_to_kept():
    row, col = iota((2 * LANES, 2 * LANES), 0), iota((2 * LANES, 2 * LANES), 1)
    w, p, c = row // LANES, row // B % 2, row % B
    return one_hot(p * LANES + w * B + kept_column(c) == col)


def blocks_first(order_ref, base, count, slots):
    col, row = iota((8, 8 * slots), 1), iota((8, 8 * slots), 0)
    same = col // slots == row
    slot = col % slots
    parts = [
        jnp.where(same & (slot == order_ref[base + k]), 1.0, 0.0) for k in range(count)
    ]
    return jnp.concatenate(parts, axis=0).astype(BF16)


def slots_last(order_ref, slots):
    n = 8 * slots
    place = iota((1, n), 1) // 8
    slot = jnp.zeros((1, n), jnp.int32)
    for k in range(slots):
        slot = jnp.where(place == k, order_ref[k], slot)
    row, col = iota((n, n), 0), iota((n, n), 1)
    return one_hot((row // slots == col % 8) & (row % slots == slot))


def inside(rows, cols):
    lane = iota((HALF, LANES), 1)
    a = 2 * iota((HALF, LANES), 0) + lane // B
    kept = lane % B
    c = 2 * (kept % HALF) + kept // HALF
    return jnp.where((a.astype(F32) < rows) & (c.astype(F32) < cols), 1.0, 0.0)


def total_of(x):
    return jnp.sum(jnp.sum(x, axis=0, keepdims=True), axis=1, keepdims=True)


def wide(x):
    return jnp.broadcast_to(x, (1, LANES))


def split(x):
    high = x.astype(BF16)
    return high, (x - high.astype(F32)).astype(BF16)


def split_three(x):
    high, _ = split(x)
    rest = x - high.astype(F32)
    middle, low = split(rest)
    return high, middle, low


def call(kernel, name, out_shape, operands, kinds, scratch=(), out_kinds=None, cost=2.0, limit=VMEM_LIMIT,
         compute=False):
    space = {"s": pltpu.SMEM, "v": pltpu.VMEM, "h": pltpu.HBM, "a": pl.ANY}
    out_kinds = out_kinds or "v" * len(out_shape)
    return pl.pallas_call(
        kernel,
        out_shape=out_shape,
        in_specs=[pl.BlockSpec(memory_space=space[k]) for k in kinds],
        out_specs=tuple(pl.BlockSpec(memory_space=space[k]) for k in out_kinds),
        scratch_shapes=list(scratch),
        compiler_params=pltpu.CompilerParams(vmem_limit_bytes=limit),
        cost_estimate=pl.CostEstimate(
            flops=int(cost * 1.0e9) if compute else 0,
            bytes_accessed=1024 if compute else int(cost * 3.0e6),
            transcendentals=0,
        ),
        name=name,
    )(*operands)


def sort_slots(core, meta_ref, order_ref, seen):
    slots = order_ref.shape[0]
    nodes = seen.shape[0]
    cap = slots // nodes
    for o in range(nodes):
        seen[o] = 0
    for j in range(slots):
        o = meta_ref[0, j]
        rank = seen[o]
        seen[o] = rank + 1
        place = o * cap + rank + core * (slots // 2)
        order_ref[jnp.where(place >= slots, place - slots, place)] = j


def arrange_kernel(masked, order_ref, meta_ref, env_ref, _, *outs):
    chans, slots = env_ref.shape[:2]
    cap = outs[0].shape[0]
    first = blocks_first(order_ref, 0, slots, slots)
    second = pair_to_kept()
    low = iota((1, 2 * LANES), 1) % LANES < B
    blank = jnp.zeros((slots, LANES), BF16)
    for g in range(4):
        used = [w for w in (2 * g, 2 * g + 1) if w < chans]
        chunks = []
        for c in range(4):
            rows = []
            for i in range(8 * c, 8 * c + 8):
                parts = [env_ref[w, :, i * LANES : (i + 1) * LANES] for w in used]
                rows.append(jnp.concatenate(parts + [blank] * (2 - len(used)), axis=1))
            x = jnp.concatenate(rows, axis=0)
            x = jnp.dot(first, x, preferred_element_type=F32).astype(BF16)
            chunks.append(jnp.dot(x, second, preferred_element_type=F32))
        for k in range(slots):
            x = jnp.concatenate([chunk[8 * k : 8 * k + 8] for chunk in chunks], axis=0)
            if masked:
                slot = order_ref[k]
                kept = [meta_ref[3 + w, slot].astype(F32) for w in used]
                x = x * jnp.where(low, kept[0], kept[-1])
            x = x.astype(BF16)
            for p in range(2):
                outs[k // cap][k % cap, p * HALF : (p + 1) * HALF, g * LANES : (g + 1) * LANES] = x[
                    :, p * LANES : (p + 1) * LANES
                ]


def ship_kernel(meta_ref, start_ref, order_ref, near_ref, far_ref, home_ref, seen):
    sort_slots(position()[1], meta_ref, order_ref, seen)
    slots = start_ref.shape[0]
    cap = slots // 4
    first = blocks_first(order_ref, 0, slots, slots)
    second = to_kept()
    chunks = []
    for c in range(4):
        rows = [start_ref[:, i * LANES : (i + 1) * LANES] for i in range(8 * c, 8 * c + 8)]
        x = jnp.dot(first, jnp.concatenate(rows, axis=0), preferred_element_type=F32).astype(BF16)
        chunks.append(jnp.dot(x, second, preferred_element_type=F32))
    halves = []
    for k in range(slots):
        slot = order_ref[k]
        x = jnp.concatenate([chunk[8 * k : 8 * k + 8] for chunk in chunks], axis=0)
        x = x * inside(meta_ref[1, slot].astype(F32), meta_ref[2, slot].astype(F32))
        home_ref[HALF * k : HALF * (k + 1), :] = x.astype(BF16)
        if k < 2 * cap:
            (near_ref, far_ref)[k // cap][HALF * (k % cap) : HALF * (k % cap + 1), :] = x.astype(BF16)
        if k % (2 * cap) == 0:
            halves.append(x * x)
        else:
            halves[-1] = halves[-1] + x * x
    squares = wide(total_of(halves[0]) + total_of(halves[1]))
    pieces = [v.astype(F32) for v in split_three(squares)]
    blank = jnp.zeros((2 * 16 - 2 * cap - 3, LANES), F32)
    for t, ref in enumerate((near_ref, far_ref)):
        lines = []
        for d in range(2):
            for k in range(cap):
                lines.append(jnp.full((1, LANES), meta_ref[1 + d, order_ref[t * cap + k]].astype(F32)))
        ref[HALF * cap :, :] = jnp.concatenate(lines + pieces + [blank], axis=0).astype(BF16)


def note(ref):
    return ref[ref.shape[0] - 32 :, :].astype(F32)


def sums_kernel(near_ref, far_ref, _, out_ref):
    lines = []
    for ref in (near_ref, far_ref):
        n = note(ref)
        lines.append(n[16:17] + n[17:18] + n[18:19])
    out_ref[...] = jnp.concatenate(lines + [jnp.zeros((6, LANES), F32)], axis=0)


BITS = 14


def encode(s, x, out_ref):
    largest = jnp.max(jnp.max(jnp.abs(x), axis=0, keepdims=True), axis=1, keepdims=True)
    power = wide(jnp.ceil(jnp.log2(jnp.maximum(largest, 1e-30))))
    code = jnp.floor(x * jnp.exp2(BITS - power) + 0.5)
    out_ref[HALF * s : HALF * (s + 1), :] = code.astype(jnp.int32).astype(jnp.int16)
    return power


def encode_end(powers, out_ref):
    cap = len(powers)
    tail = jnp.concatenate(powers + [jnp.zeros((16 - cap, LANES), F32)], axis=0)
    out_ref[HALF * cap :, :] = tail.astype(jnp.int32).astype(jnp.int16)


def decode(ref, s, scales):
    return ref[HALF * s : HALF * (s + 1), :].astype(jnp.int32).astype(F32) * scales[s : s + 1]


def decode_scales(ref):
    return jnp.exp2(ref[ref.shape[0] - 16 :, :].astype(jnp.int32).astype(F32) - BITS)


def block_diagonal(x):
    low = iota((HALF, LANES), 1) < B
    swapped = pltpu.roll(x, B, 1)
    zero = jnp.zeros_like(x)
    two = jnp.concatenate(
        [
            jnp.where(low, x, zero),
            jnp.where(low, swapped, zero),
            jnp.where(low, zero, swapped),
            jnp.where(low, zero, x),
        ],
        axis=0,
    )
    blank = jnp.zeros_like(two)
    return jnp.concatenate(
        [jnp.concatenate([two, blank], axis=1), jnp.concatenate([blank, two], axis=1)], axis=0
    )


def product(q_ref, envs, y_ref, inner_ref, rounded):
    count = q_ref.shape[0]
    span = 2 * LANES
    keep_left, keep_right, got_left, got_right = envs
    for s in range(count):
        high, low = split(block_diagonal(q_ref[s]))
        left = jnp.concatenate(
            [ref[s, :, g * span : (g + 1) * span] for ref in (keep_left, got_left) for g in range(2)], axis=0
        )
        inner = jnp.dot(left, high, preferred_element_type=F32)
        if not rounded:
            inner = inner + jnp.dot(left, low, preferred_element_type=F32)
        high, low = split(inner)
        for k in range(4):
            inner_ref[s, :B, k * span : (k + 1) * span] = high[k * B : (k + 1) * B]
            inner_ref[s, B:, k * span : (k + 1) * span] = low[k * B : (k + 1) * B]
    powers = []
    for s in range(count):
        right = jnp.concatenate([keep_right[s], got_right[s]], axis=1)
        both = lax.dot_general(inner_ref[s], right, (((1,), (1,)), ((), ())), preferred_element_type=F32)
        image = both[:B] + both[B:]
        powers.append(encode(s, jnp.concatenate([image[:HALF], image[HALF:]], axis=1), y_ref))
    encode_end(powers, y_ref)


def start_kernel(count, nodes, ship_ref, sums_ref, more_ref, *refs):
    envs, (q_ref, y_ref, scale_ref, inner_ref) = refs[:4], refs[4:]
    node, core = position()
    by_node = []
    for e in range(nodes):
        value = jnp.zeros((1, LANES), F32)
        for ref, c in ((sums_ref, core), (more_ref, 1 - core)):
            for t in range(2):
                source = lax.rem(node + 2 * nodes - 2 * c - t, nodes)
                value = value + jnp.where(source == e, ref[t : t + 1, :], 0.0)
        by_node.append(value)
    squares = (by_node[0] + by_node[1]) + (by_node[2] + by_node[3])
    scale = 1.0 / jnp.sqrt(squares / count + 1e-06)
    scale_ref[...] = jnp.broadcast_to(scale, scale_ref.shape)
    for s in range(q_ref.shape[0]):
        q_ref[s] = ship_ref[HALF * s : HALF * (s + 1), :].astype(F32) * scale
    product(q_ref, envs, y_ref, inner_ref, True)


def orthogonal(ship_ref, own_ref, other_ref, basis, q_ref):
    n = note(ship_ref)
    cap = q_ref.shape[0]
    ahead = lax.axis_index("op") < 2
    own_scales, other_scales = decode_scales(own_ref), decode_scales(other_ref)
    for s in range(cap):
        own, other = decode(own_ref, s, own_scales), decode(other_ref, s, other_scales)
        image = jnp.where(ahead, own, other) + jnp.where(ahead, other, own)
        q_ref[s] = image * inside(n[s : s + 1], n[cap + s : cap + s + 1])
    image = q_ref[...].reshape(cap * HALF, LANES)
    rows = []
    rest = image
    for ref in basis:
        q = ref[...].reshape(cap * HALF, LANES)
        length = total_of(q * q)
        along = total_of(q * image)
        row = wide(jnp.where(length > 0, along / jnp.where(length > 0, length, 1.0), 0.0))
        rest = rest - row * q
        rows.append(row)
    q_ref[...] = rest.reshape(q_ref.shape)
    return rows


def step_kernel(count, *refs):
    ship_ref, own_ref, other_ref = refs[:3]
    basis = refs[3 : 3 + count]
    envs = refs[3 + count : 7 + count]
    q_ref, y_ref, along_ref, *parcel_ref, inner_ref = refs[7 + count :]
    rows = orthogonal(ship_ref, own_ref, other_ref, basis, q_ref)
    along_ref[...] = jnp.concatenate(rows + [jnp.zeros((8 - count, LANES), F32)], axis=0)
    for ref in parcel_ref:
        vectors = [r[...].reshape(-1, LANES) for r in (*basis[1:], q_ref)]
        ref[...] = jnp.concatenate(vectors, axis=0).astype(BF16)
    product(q_ref, envs, y_ref, inner_ref, False)


def line_of(values):
    lane = iota((1, LANES), 1)
    line = jnp.zeros((1, LANES), F32)
    for k, value in enumerate(values):
        line = jnp.where(lane == k, value, line)
    return line


def table_kernel(*refs):
    out_refs, table_ref = refs[16:18], refs[18]
    lines = []
    for t in range(2):
        ship_ref, own_ref, other_ref, q0, q1, q2, c1, c2 = refs[8 * t : 8 * t + 8]
        last = orthogonal(ship_ref, own_ref, other_ref, (q0, q1, q2), out_refs[t])
        vectors = [ref[...].reshape(-1, LANES) for ref in (q0, q1, q2, out_refs[t])]
        values = [total_of(vectors[i] * vectors[j]) for i in range(4) for j in range(i, 4)]
        lines.append(line_of(values + [c1[0:1], c2[0:1], c2[1:2]] + last))
    table_ref[...] = jnp.concatenate(lines + [jnp.zeros((6, LANES), F32)], axis=0)


def pack_kernel(table_ref, other_ref, *refs):
    core = position()[1]
    mine, other = table_ref[0:2, :], other_ref[0:2, :]
    lines = jnp.concatenate([jnp.where(core == 0, mine, other), jnp.where(core == 0, other, mine)], axis=0)
    pieces = [v.astype(F32) for v in split_three(lines)]
    tail = jnp.concatenate(pieces + [jnp.zeros((4, LANES), F32)], axis=0).astype(BF16)
    for ref, out_ref in zip(refs[:2], refs[2:]):
        rows = ref.shape[0] * HALF
        out_ref[:rows, :] = ref[...].reshape(rows, LANES).astype(BF16)
        out_ref[rows:, :] = tail


def combine(count, take):
    gram = {}
    row = 0
    for i in range(4):
        for j in range(i, 4):
            gram[i, j] = gram[j, i] = take(row)
            row += 1
    one = jnp.ones_like(gram[0, 0])
    images = [
        [take(10), one, None, None],
        [take(11), take(12), one, None],
        [take(13), take(14), take(15), one],
    ]

    def mean(u, v):
        acc = None
        for i in range(4):
            for j in range(4):
                if u[i] is not None and v[j] is not None:
                    term = u[i] * v[j] * gram[i, j]
                    acc = term if acc is None else acc + term
        return jnp.sum(acc, axis=0, keepdims=True) / count

    basis = [[one, None, None, None]]
    projections = {}
    for k in range(ITERS):
        image = [None] * 4
        for z, parts in zip(basis[k], images):
            for m, v in enumerate(parts):
                if z is not None and v is not None:
                    image[m] = z * v if image[m] is None else image[m] + z * v
        rest = list(image)
        for i in range(k + 1):
            p = mean(basis[i], image)
            projections[i, k] = p
            for m, v in enumerate(basis[i]):
                if v is not None:
                    rest[m] = rest[m] - p * v
        if k + 1 < ITERS:
            scale = 1.0 / jnp.sqrt(mean(rest, rest) + 1e-06)
            basis.append([None if v is None else v * scale for v in rest])
    return projections, rest


def finish_kernel(count, nodes, order_ref, scale_ref, home_ref, *refs):
    early, late, (out_ref, proj_ref) = refs[:4], refs[4:8], refs[8:]
    node, core = position()
    slots = out_ref.shape[0]
    rows = home_ref.shape[0] // 4
    sources = []
    lines = [jnp.zeros((4, LANES), F32) for _ in range(nodes)]
    for k, ref in enumerate(late):
        hop = 2 * (core if k < 2 else 1 - core) + k % 2
        host = lax.rem(node + hop, nodes)
        tail = ref[rows:, :].astype(F32)
        four = tail[0:4] + tail[4:8] + tail[8:12]
        lines = [jnp.where(host == e, four, v) for e, v in enumerate(lines)]
        sources.append((early[k], ref, host * 4 + hop))
    table = jnp.concatenate(lines, axis=0)
    sets = 4 * nodes
    projections, rest = combine(
        count, lambda k: jnp.broadcast_to(table[:, k : k + 1], (sets, LANES)))
    lines = [line_of([projections.get((i, k), 0.0) for k in range(ITERS)]) for i in range(ITERS)]
    proj_ref[...] = jnp.concatenate(lines, axis=0)[:, :ITERS]
    scale = scale_ref[0:1, :]
    blocks = []
    for k, (two, one, index) in enumerate(sources):
        mine = iota((sets, LANES), 0) == index
        coeff = [jnp.sum(jnp.where(mine, v, 0.0), axis=0, keepdims=True) for v in rest]
        x = coeff[0] * (home_ref[rows * k : rows * (k + 1), :].astype(F32) * scale)
        x = x + coeff[1] * two[:rows, :].astype(F32) + coeff[2] * two[rows:, :].astype(F32)
        x = x + coeff[3] * one[:rows, :].astype(F32)
        blocks.append(x)
    first = slots_last(order_ref, slots)
    second = from_kept_twice()
    per = rows // HALF
    for c in range(4):
        x = jnp.concatenate(
            [blocks[k // per][HALF * (k % per) + 8 * c : HALF * (k % per) + 8 * c + 8] for k in range(slots)],
            axis=0,
        )
        x = jnp.dot(first, jnp.concatenate(split(x), axis=1), preferred_element_type=F32).astype(BF16)
        x = jnp.dot(x, second, preferred_element_type=F32)
        for i in range(8):
            out_ref[:, (8 * c + i) * LANES : (8 * c + i + 1) * LANES] = x[i * slots : (i + 1) * slots]


def paired(start_vector, extents, offsets, env_left, env_right, channel_mask):
    nodes = lax.axis_size("sector")
    ops = lax.axis_size("op")
    slots = start_vector.shape[0]
    cap = slots // nodes
    count = float(slots * nodes * B * B)
    swap_core = [(i, i ^ 1) for i in range(ops)]
    swap_x = [(i, i ^ 2) for i in range(ops)]
    left = jnp.transpose(env_left, (1, 0, 2))
    right = jnp.transpose(env_right, (1, 0, 2))
    meta = jnp.concatenate([offsets[None], jnp.transpose(extents), jnp.transpose(channel_mask)], axis=0)

    def route(t, back):
        pairs = []
        for h in range(nodes):
            for q in range(ops):
                to = (h + 2 * (q % 2) + t) % nodes
                a, b = h * ops + q, to * ops + q
                pairs.append((b, a) if back else (a, b))
        return pairs

    def across(x):
        return lax.ppermute(x, "op", swap_core)

    def shape(dims, dtype=F32):
        return jax.ShapeDtypeStruct(dims, dtype)

    environment = shape((cap, B, WIDE), BF16)
    vector = shape((cap, HALF, LANES))
    tile = shape((8, LANES))
    code = shape((cap * HALF + 16, LANES), jnp.int16)
    payload = shape((cap * HALF + 32, LANES), BF16)
    order, *ships, home = call(
        ship_kernel, "ship",
        (shape((slots,), jnp.int32), payload, payload, shape((slots * HALF, LANES), BF16)),
        (meta, start_vector), "sv", [pltpu.SMEM((nodes,), jnp.int32)], "svvv", 2.0, ROOMY, True)
    ships = [lax.ppermute(x, ("sector", "op"), route(t, False)) for t, x in enumerate(ships)]

    def arrange(masked, env, after):
        sets = call(
            lambda *refs: arrange_kernel(masked, *refs), "arrange", (environment,) * 4, (order, meta, env, after),
            "ssva", cost=3.0, limit=ARRANGE, compute=True)
        return sets[:2], [across(x) for x in sets[2:]]

    keep_left, got_left = arrange(True, left, order)
    (sums,) = call(sums_kernel, "sums", (tile,), (*ships, keep_left[0]), "vva", cost=0.3)
    keep_right, got_right = arrange(False, right, sums)
    envs = [(keep_left[t], keep_right[t], got_left[t], got_right[t]) for t in range(2)]
    more = across(sums)

    def start(*refs):
        start_kernel(count, nodes, *refs)

    def step(k):
        return lambda *refs: step_kernel(k, *refs)

    inner = [pltpu.VMEM((cap, LANES, 2 * WIDE), BF16)]
    basis = [[], []]
    along = [[], []]
    images = [None, None]
    early = []
    for t in range(2):
        q, y, scale = call(
            start, "first", (vector, code, tile), (ships[t], sums, more, *envs[t]), "v" * 7, inner)
        basis[t].append(q)
        images[t] = (y, lax.ppermute(y, "op", swap_x))
    for k in range(1, ITERS):
        for t in range(2):
            outs = [vector, code, tile]
            if k == ITERS - 1:
                outs.append(shape((2 * cap * HALF, LANES), BF16))
            q, y, a, *parcel = call(
                step(k), ("second", "third")[k - 1], tuple(outs),
                (ships[t], *images[t], *basis[t], *envs[t]), "v" * (7 + k), inner)
            basis[t].append(q)
            along[t].append(a)
            images[t] = (y, lax.ppermute(y, "op", swap_x))
            early += [lax.ppermute(x, ("sector", "op"), route(t, True)) for x in parcel]
    early += [across(x) for x in early]

    operands = []
    for t in range(2):
        operands += [ships[t], *images[t], *basis[t], *along[t]]
    *last, table = call(table_kernel, "table", (vector, vector, tile), operands, "v" * 16, cost=1.0)
    parcel = shape((cap * HALF + 16, LANES), BF16)
    late = call(
        pack_kernel, "pack", (parcel, parcel), (table, across(table), *last), "vvvv", cost=0.7)
    late = [lax.ppermute(x, ("sector", "op"), route(t, True)) for t, x in enumerate(late)]
    late += [across(x) for x in late]

    def finish(*refs):
        finish_kernel(count, nodes, *refs)

    return call(
        finish, "finish", (shape((slots, B * B)), shape((ITERS, ITERS))),
        (order, scale, home, *early, *late), "s" + "v" * 10)


def pack_rows(data, index, nodes, cap):
    slots = data.shape[0]
    hit = jnp.arange(nodes * cap, dtype=jnp.int32)[:, None] == index[None, :]
    source = jnp.sum(jnp.where(hit, jnp.arange(slots, dtype=jnp.int32)[None, :], 0), axis=1)
    filled = jnp.any(hit, axis=1)
    rows = jnp.take(data, source, axis=0)
    rows = jnp.where(filled[:, None], rows, jnp.zeros_like(rows))
    return rows.reshape(nodes, cap, data.shape[1])


def unpack_rows(arrived, index):
    flat = arrived.reshape(arrived.shape[0] * arrived.shape[1], arrived.shape[2])
    return jnp.take(flat, index, axis=0)


def general(start_vector, extents, offsets, env_left, env_right, channel_mask):
    nodes = lax.axis_size("sector")
    here_index = lax.axis_index("sector")
    slots = start_vector.shape[0]
    cap = max(1, slots // nodes)
    chans = env_left.shape[1]
    count = float(slots * nodes * B * B)
    slot_ids = jnp.arange(slots, dtype=jnp.int32)
    same = offsets[:, None] == offsets[None, :]
    earlier = slot_ids[None, :] < slot_ids[:, None]
    rank = jnp.sum((same & earlier).astype(jnp.int32), axis=1)
    send_index = (here_index + offsets) % nodes * cap + rank
    recv_index = (here_index - offsets) % nodes * cap + rank
    position = jnp.arange(B * B, dtype=jnp.int32)
    inside = ((position // B)[None, :] < extents[:, 0:1]) & (
        (position % B)[None, :] < extents[:, 1:2]
    )
    mask = inside.astype(jnp.float32)
    left = env_left.reshape(slots, chans, B, B)
    right_wide = env_right.reshape(slots, chans, B, B).astype(jnp.float32)
    chan = channel_mask.astype(jnp.float32)

    def squares(vector):
        return lax.psum(jnp.sum(vector * vector), "sector") / count

    def correlation_table(basis, image):
        local = [jnp.sum(vector * image) for vector in basis]
        local = local + [jnp.zeros((), jnp.float32)] * (ITERS - len(basis))
        return lax.psum(jnp.stack(local), "sector") / count

    masked = mask * start_vector.astype(jnp.float32)
    basis = [masked / jnp.sqrt(squares(masked) + 1e-06)]
    projections = jnp.zeros((ITERS, ITERS), jnp.float32)
    residual = masked
    for step in range(ITERS):
        moving = pack_rows(basis[step].astype(jnp.bfloat16), send_index, nodes, cap)
        arrived = lax.all_to_all(moving, "sector", split_axis=0, concat_axis=0, tiled=True)
        blocks = unpack_rows(arrived, recv_index).reshape(slots, B, B)
        inner = jnp.einsum("swab,sbc->swac", left, blocks, preferred_element_type=jnp.float32)
        inner = inner * chan[:, :, None, None]
        partial_image = jnp.einsum(
            "swac,swdc->sad", inner, right_wide, precision=lax.Precision.HIGHEST
        )
        total = lax.psum(partial_image.reshape(slots, B * B), "op")
        going = pack_rows(total, recv_index, nodes, cap)
        returned = lax.all_to_all(going, "sector", split_axis=0, concat_axis=0, tiled=True)
        apply_image = unpack_rows(returned, send_index)
        image = apply_image * mask
        coeffs = correlation_table(basis, image)
        residual = image
        for index in range(step + 1):
            projections = projections.at[index, step].set(coeffs[index])
            residual = residual - coeffs[index] * basis[index]
        if step + 1 < ITERS:
            basis.append(residual / jnp.sqrt(squares(residual) + 1e-06))
    return (residual, projections)


def solution(mesh):
    def on_device(start_vector, extents, offsets, env_left, env_right, channel_mask):
        nodes, ops = mesh.shape["sector"], mesh.shape["op"]
        slots, chans = env_left.shape[:2]
        fits = nodes == 4 and ops == 4 and slots == 8 * nodes and chans <= 8
        body = paired if fits else general
        return body(start_vector, extents, offsets, env_left, env_right, channel_mask)

    return jax.shard_map(
        on_device,
        mesh=mesh,
        in_specs=(
            P(("groups", "sector"), None),
            P(("groups", "sector"), None),
            P("groups"),
            P(("groups", "sector"), "op", None),
            P(("groups", "sector"), "op", None),
            P(("groups", "sector"), "op"),
        ),
        out_specs=(P(("groups", "sector"), None), P("groups", None)),
        check_vma=False,
    )
```

```python
import jax
import jax.numpy as jnp
from jax import lax
from jax.experimental import pallas as pl
from jax.experimental.pallas import tpu as pltpu
from jax.sharding import PartitionSpec as P

B = 64
ITERS = 3
HALF = 32
LANES = 128
WIDE = 4 * LANES
F32 = jnp.float32
BF16 = jnp.bfloat16
VMEM_LIMIT = 24 * 1024 * 1024
ROOMY = 32 * 1024 * 1024
ARRANGE = 32 * 1024 * 1024


def position():
    return lax.axis_index("sector"), lax.axis_index("op") % 2


def iota(shape, dim):
    return lax.broadcasted_iota(jnp.int32, shape, dim)


def one_hot(condition):
    return jnp.where(condition, 1.0, 0.0).astype(BF16)


def kept_column(c):
    return (c % 2) * HALF + c // 2


def to_kept():
    row, col = iota((LANES, LANES), 0), iota((LANES, LANES), 1)
    return one_hot(row // B * B + kept_column(row % B) == col)


def from_kept_twice():
    row, col = iota((2 * LANES, LANES), 0) % LANES, iota((2 * LANES, LANES), 1)
    return one_hot(col // B * B + kept_column(col % B) == row)


def pair_to_kept():
    row, col = iota((2 * LANES, 2 * LANES), 0), iota((2 * LANES, 2 * LANES), 1)
    w, p, c = row // LANES, row // B % 2, row % B
    return one_hot(p * LANES + w * B + kept_column(c) == col)


def blocks_first(order_ref, base, count, slots):
    col, row = iota((8, 8 * slots), 1), iota((8, 8 * slots), 0)
    same = col // slots == row
    slot = col % slots
    parts = [
        jnp.where(same & (slot == order_ref[base + k]), 1.0, 0.0) for k in range(count)
    ]
    return jnp.concatenate(parts, axis=0).astype(BF16)


def slots_last(order_ref, slots):
    n = 8 * slots
    place = iota((1, n), 1) // 8
    slot = jnp.zeros((1, n), jnp.int32)
    for k in range(slots):
        slot = jnp.where(place == k, order_ref[k], slot)
    row, col = iota((n, n), 0), iota((n, n), 1)
    return one_hot((row // slots == col % 8) & (row % slots == slot))


def inside(rows, cols):
    lane = iota((HALF, LANES), 1)
    a = 2 * iota((HALF, LANES), 0) + lane // B
    kept = lane % B
    c = 2 * (kept % HALF) + kept // HALF
    return jnp.where((a.astype(F32) < rows) & (c.astype(F32) < cols), 1.0, 0.0)


def total_of(x):
    return jnp.sum(jnp.sum(x, axis=0, keepdims=True), axis=1, keepdims=True)


def wide(x):
    return jnp.broadcast_to(x, (1, LANES))


def split(x):
    high = x.astype(BF16)
    return high, (x - high.astype(F32)).astype(BF16)


def split_three(x):
    high, _ = split(x)
    rest = x - high.astype(F32)
    middle, low = split(rest)
    return high, middle, low


def call(kernel, name, out_shape, operands, kinds, scratch=(), out_kinds=None, cost=2.0, limit=VMEM_LIMIT,
         compute=False):
    space = {"s": pltpu.SMEM, "v": pltpu.VMEM, "h": pltpu.HBM, "a": pl.ANY}
    out_kinds = out_kinds or "v" * len(out_shape)
    return pl.pallas_call(
        kernel,
        out_shape=out_shape,
        in_specs=[pl.BlockSpec(memory_space=space[k]) for k in kinds],
        out_specs=tuple(pl.BlockSpec(memory_space=space[k]) for k in out_kinds),
        scratch_shapes=list(scratch),
        compiler_params=pltpu.CompilerParams(vmem_limit_bytes=limit),
        cost_estimate=pl.CostEstimate(
            flops=int(cost * 1.0e9) if compute else 0,
            bytes_accessed=1024 if compute else int(cost * 3.0e6),
            transcendentals=0,
        ),
        name=name,
    )(*operands)


def sort_slots(core, meta_ref, order_ref, seen):
    slots = order_ref.shape[0]
    nodes = seen.shape[0]
    cap = slots // nodes
    for o in range(nodes):
        seen[o] = 0
    for j in range(slots):
        o = meta_ref[0, j]
        rank = seen[o]
        seen[o] = rank + 1
        place = o * cap + rank + core * (slots // 2)
        order_ref[jnp.where(place >= slots, place - slots, place)] = j


def note(ref):
    return ref[ref.shape[0] - 32 :, :].astype(F32)


def arrived_kernel(near_in_ref, far_in_ref, _, near_ref, far_ref):
    near_ref[...] = near_in_ref[...]
    far_ref[...] = far_in_ref[...]


def riding_sums(ships):
    pieces = [note(ref)[16:19] for ref in ships]
    tile = jnp.concatenate(pieces + [jnp.zeros((HALF - 6, LANES), F32)], axis=0)
    tile = jnp.where(iota((HALF, LANES), 1) >= B, tile, 0.0)
    return jnp.concatenate([tile, jnp.zeros_like(tile)], axis=1)


def arrange_kernel(order_ref, meta_ref, env_ref, *refs):
    ships, outs = refs[:-4], refs[-4:]
    masked = not ships
    if ships:
        riding = riding_sums(ships)
    chans, slots = env_ref.shape[:2]
    cap = outs[0].shape[0]
    first = blocks_first(order_ref, 0, slots, slots)
    second = pair_to_kept()
    low = iota((1, 2 * LANES), 1) % LANES < B
    blank = jnp.zeros((slots, LANES), BF16)
    for g in range(4):
        used = [w for w in (2 * g, 2 * g + 1) if w < chans]
        chunks = []
        for c in range(4):
            rows = []
            for i in range(8 * c, 8 * c + 8):
                parts = [env_ref[w, :, i * LANES : (i + 1) * LANES] for w in used]
                rows.append(jnp.concatenate(parts + [blank] * (2 - len(used)), axis=1))
            x = jnp.concatenate(rows, axis=0)
            x = jnp.dot(first, x, preferred_element_type=F32).astype(BF16)
            chunks.append(jnp.dot(x, second, preferred_element_type=F32))
        for k in range(slots):
            x = jnp.concatenate([chunk[8 * k : 8 * k + 8] for chunk in chunks], axis=0)
            if masked:
                slot = order_ref[k]
                kept = [meta_ref[3 + w, slot].astype(F32) for w in used]
                x = x * jnp.where(low, kept[0], kept[-1])
            elif g == 3 and k in (2 * cap, 3 * cap):
                x = x + riding
            x = x.astype(BF16)
            for p in range(2):
                outs[k // cap][k % cap, p * HALF : (p + 1) * HALF, g * LANES : (g + 1) * LANES] = x[
                    :, p * LANES : (p + 1) * LANES
                ]


def ship_kernel(meta_ref, start_ref, order_ref, near_ref, far_ref, home_ref, seen):
    sort_slots(position()[1], meta_ref, order_ref, seen)
    slots = start_ref.shape[0]
    cap = slots // 4
    first = blocks_first(order_ref, 0, slots, slots)
    second = to_kept()
    chunks = []
    for c in range(4):
        rows = [start_ref[:, i * LANES : (i + 1) * LANES] for i in range(8 * c, 8 * c + 8)]
        x = jnp.dot(first, jnp.concatenate(rows, axis=0), preferred_element_type=F32).astype(BF16)
        chunks.append(jnp.dot(x, second, preferred_element_type=F32))
    halves = []
    for k in range(slots):
        slot = order_ref[k]
        x = jnp.concatenate([chunk[8 * k : 8 * k + 8] for chunk in chunks], axis=0)
        x = x * inside(meta_ref[1, slot].astype(F32), meta_ref[2, slot].astype(F32))
        home_ref[HALF * k : HALF * (k + 1), :] = x.astype(BF16)
        if k < 2 * cap:
            (near_ref, far_ref)[k // cap][HALF * (k % cap) : HALF * (k % cap + 1), :] = x.astype(BF16)
        if k % (2 * cap) == 0:
            halves.append(x * x)
        else:
            halves[-1] = halves[-1] + x * x
    squares = wide(total_of(halves[0]) + total_of(halves[1]))
    pieces = [v.astype(F32) for v in split_three(squares)]
    blank = jnp.zeros((2 * 16 - 2 * cap - 3, LANES), F32)
    for t, ref in enumerate((near_ref, far_ref)):
        lines = []
        for d in range(2):
            for k in range(cap):
                lines.append(jnp.full((1, LANES), meta_ref[1 + d, order_ref[t * cap + k]].astype(F32)))
        ref[HALF * cap :, :] = jnp.concatenate(lines + pieces + [blank], axis=0).astype(BF16)


BITS = 14


def encode(s, x, out_ref):
    largest = jnp.max(jnp.max(jnp.abs(x), axis=0, keepdims=True), axis=1, keepdims=True)
    power = wide(jnp.ceil(jnp.log2(jnp.maximum(largest, 1e-30))))
    code = jnp.floor(x * jnp.exp2(BITS - power) + 0.5)
    out_ref[HALF * s : HALF * (s + 1), :] = code.astype(jnp.int32).astype(jnp.int16)
    return power


def encode_end(powers, out_ref):
    cap = len(powers)
    tail = jnp.concatenate(powers + [jnp.zeros((16 - cap, LANES), F32)], axis=0)
    out_ref[HALF * cap :, :] = tail.astype(jnp.int32).astype(jnp.int16)


def decode(ref, s, scales):
    return ref[HALF * s : HALF * (s + 1), :].astype(jnp.int32).astype(F32) * scales[s : s + 1]


def decode_scales(ref):
    return jnp.exp2(ref[ref.shape[0] - 16 :, :].astype(jnp.int32).astype(F32) - BITS)


def block_diagonal(x):
    low = iota((HALF, LANES), 1) < B
    swapped = pltpu.roll(x, B, 1)
    zero = jnp.zeros_like(x)
    two = jnp.concatenate(
        [
            jnp.where(low, x, zero),
            jnp.where(low, swapped, zero),
            jnp.where(low, zero, swapped),
            jnp.where(low, zero, x),
        ],
        axis=0,
    )
    blank = jnp.zeros_like(two)
    return jnp.concatenate(
        [jnp.concatenate([two, blank], axis=1), jnp.concatenate([blank, two], axis=1)], axis=0
    )


def product(q_ref, envs, y_ref, inner_ref, rounded):
    count = q_ref.shape[0]
    span = 2 * LANES
    keep_left, keep_right, got_left, got_right = envs
    for s in range(count):
        high, low = split(block_diagonal(q_ref[s]))
        left = jnp.concatenate(
            [ref[s, :, g * span : (g + 1) * span] for ref in (keep_left, got_left) for g in range(2)], axis=0
        )
        inner = jnp.dot(left, high, preferred_element_type=F32)
        if not rounded:
            inner = inner + jnp.dot(left, low, preferred_element_type=F32)
        high, low = split(inner)
        for k in range(4):
            inner_ref[s, :B, k * span : (k + 1) * span] = high[k * B : (k + 1) * B]
            inner_ref[s, B:, k * span : (k + 1) * span] = low[k * B : (k + 1) * B]
    powers = []
    for s in range(count):
        right = jnp.concatenate([keep_right[s], got_right[s]], axis=1)
        both = lax.dot_general(inner_ref[s], right, (((1,), (1,)), ((), ())), preferred_element_type=F32)
        image = both[:B] + both[B:]
        powers.append(encode(s, jnp.concatenate([image[:HALF], image[HALF:]], axis=1), y_ref))
    encode_end(powers, y_ref)


def start_kernel(count, nodes, t, *refs):
    ships, envs, (q_ref, y_ref, scale_ref, inner_ref) = refs[:2], refs[2:6], refs[6:]
    node, core = position()
    ship_ref = ships[t]
    mine = [note(ref)[16:19] for ref in ships]
    tile = envs[3][0, :HALF, WIDE - LANES :].astype(F32)
    tile = jnp.where(iota((HALF, LANES), 1) >= B, tile, pltpu.roll(tile, B, 1))
    theirs = [tile[0:3], tile[3:6]]
    by_node = []
    for e in range(nodes):
        value = jnp.zeros((1, LANES), F32)
        for sums, c in ((mine, core), (theirs, 1 - core)):
            for hop, p in enumerate(sums):
                source = lax.rem(node + 2 * nodes - 2 * c - hop, nodes)
                value = value + jnp.where(source == e, p[0:1] + p[1:2] + p[2:3], 0.0)
        by_node.append(value)
    squares = (by_node[0] + by_node[1]) + (by_node[2] + by_node[3])
    scale = 1.0 / jnp.sqrt(squares / count + 1e-06)
    scale_ref[...] = jnp.broadcast_to(scale, scale_ref.shape)
    for s in range(q_ref.shape[0]):
        q_ref[s] = ship_ref[HALF * s : HALF * (s + 1), :].astype(F32) * scale
    product(q_ref, envs, y_ref, inner_ref, True)


def orthogonal(ship_ref, own_ref, other_ref, basis, q_ref):
    n = note(ship_ref)
    cap = q_ref.shape[0]
    ahead = lax.axis_index("op") < 2
    own_scales, other_scales = decode_scales(own_ref), decode_scales(other_ref)
    for s in range(cap):
        own, other = decode(own_ref, s, own_scales), decode(other_ref, s, other_scales)
        image = jnp.where(ahead, own, other) + jnp.where(ahead, other, own)
        q_ref[s] = image * inside(n[s : s + 1], n[cap + s : cap + s + 1])
    image = q_ref[...].reshape(cap * HALF, LANES)
    rows = []
    rest = image
    for ref in basis:
        q = ref[...].reshape(cap * HALF, LANES)
        length = total_of(q * q)
        along = total_of(q * image)
        row = wide(jnp.where(length > 0, along / jnp.where(length > 0, length, 1.0), 0.0))
        rest = rest - row * q
        rows.append(row)
    q_ref[...] = rest.reshape(q_ref.shape)
    return rows


def step_kernel(count, *refs):
    ship_ref, own_ref, other_ref = refs[:3]
    basis = refs[3 : 3 + count]
    envs = refs[3 + count : 7 + count]
    q_ref, y_ref, along_ref, *parcel_ref, inner_ref = refs[7 + count :]
    rows = orthogonal(ship_ref, own_ref, other_ref, basis, q_ref)
    along_ref[...] = jnp.concatenate(rows + [jnp.zeros((8 - count, LANES), F32)], axis=0)
    for ref in parcel_ref:
        mine = jnp.where(lax.axis_index("op") < 2, basis[1][...], q_ref[...])
        mine = mine.reshape(-1, LANES).astype(BF16)
        blank = jnp.zeros((ref.shape[0] - mine.shape[0], LANES), BF16)
        ref[...] = jnp.concatenate([mine, blank], axis=0)
    product(q_ref, envs, y_ref, inner_ref, False)


def line_of(values):
    lane = iota((1, LANES), 1)
    line = jnp.zeros((1, LANES), F32)
    for k, value in enumerate(values):
        line = jnp.where(lane == k, value, line)
    return line


def table_kernel(*refs):
    out_refs, table_ref = refs[16:18], refs[18]
    lines = []
    for t in range(2):
        ship_ref, own_ref, other_ref, q0, q1, q2, c1, c2 = refs[8 * t : 8 * t + 8]
        last = orthogonal(ship_ref, own_ref, other_ref, (q0, q1, q2), out_refs[t])
        vectors = [ref[...].reshape(-1, LANES) for ref in (q0, q1, q2, out_refs[t])]
        values = [total_of(vectors[i] * vectors[j]) for i in range(4) for j in range(i, 4)]
        lines.append(line_of(values + [c1[0:1], c2[0:1], c2[1:2]] + last))
    table_ref[...] = jnp.concatenate(lines + [jnp.zeros((6, LANES), F32)], axis=0)


def pack_kernel(table_ref, other_ref, *refs):
    core = position()[1]
    mine, other = table_ref[0:2, :], other_ref[0:2, :]
    lines = jnp.concatenate([jnp.where(core == 0, mine, other), jnp.where(core == 0, other, mine)], axis=0)
    pieces = [v.astype(F32) for v in split_three(lines)]
    tail = jnp.concatenate(pieces + [jnp.zeros((4, LANES), F32)], axis=0).astype(BF16)
    for ref, out_ref in zip(refs[:2], refs[2:]):
        rows = ref.shape[0] * HALF
        out_ref[:rows, :] = ref[...].reshape(rows, LANES).astype(BF16)
        out_ref[rows:, :] = tail


def combine(count, take):
    gram = {}
    row = 0
    for i in range(4):
        for j in range(i, 4):
            gram[i, j] = gram[j, i] = take(row)
            row += 1
    one = jnp.ones_like(gram[0, 0])
    images = [
        [take(10), one, None, None],
        [take(11), take(12), one, None],
        [take(13), take(14), take(15), one],
    ]

    def mean(u, v):
        acc = None
        for i in range(4):
            for j in range(4):
                if u[i] is not None and v[j] is not None:
                    term = u[i] * v[j] * gram[i, j]
                    acc = term if acc is None else acc + term
        return jnp.sum(acc, axis=0, keepdims=True) / count

    basis = [[one, None, None, None]]
    projections = {}
    for k in range(ITERS):
        image = [None] * 4
        for z, parts in zip(basis[k], images):
            for m, v in enumerate(parts):
                if z is not None and v is not None:
                    image[m] = z * v if image[m] is None else image[m] + z * v
        rest = list(image)
        for i in range(k + 1):
            p = mean(basis[i], image)
            projections[i, k] = p
            for m, v in enumerate(basis[i]):
                if v is not None:
                    rest[m] = rest[m] - p * v
        if k + 1 < ITERS:
            scale = 1.0 / jnp.sqrt(mean(rest, rest) + 1e-06)
            basis.append([None if v is None else v * scale for v in rest])
    return projections, rest


def finish_kernel(count, nodes, order_ref, scale_ref, home_ref, *refs):
    early, late, (out_ref, proj_ref) = refs[:8], refs[8:12], refs[12:]
    node, core = position()
    slots = out_ref.shape[0]
    rows = home_ref.shape[0] // 4
    sources = []
    lines = [jnp.zeros((4, LANES), F32) for _ in range(nodes)]
    for k, ref in enumerate(late):
        hop = 2 * (core if k < 2 else 1 - core) + k % 2
        host = lax.rem(node + hop, nodes)
        tail = ref[rows:, :].astype(F32)
        four = tail[0:4] + tail[4:8] + tail[8:12]
        lines = [jnp.where(host == e, four, v) for e, v in enumerate(lines)]
        sources.append((*early[2 * k : 2 * k + 2], ref, host * 4 + hop))
    table = jnp.concatenate(lines, axis=0)
    sets = 4 * nodes
    projections, rest = combine(
        count, lambda k: jnp.broadcast_to(table[:, k : k + 1], (sets, LANES)))
    lines = [line_of([projections.get((i, k), 0.0) for k in range(ITERS)]) for i in range(ITERS)]
    proj_ref[...] = jnp.concatenate(lines, axis=0)[:, :ITERS]
    scale = scale_ref[0:1, :]
    blocks = []
    ahead = lax.axis_index("op") < 2
    for k, (mine_ref, more_ref, last_ref, index) in enumerate(sources):
        mine = iota((sets, LANES), 0) == index
        coeff = [jnp.sum(jnp.where(mine, v, 0.0), axis=0, keepdims=True) for v in rest]
        x = coeff[0] * (home_ref[rows * k : rows * (k + 1), :].astype(F32) * scale)
        here, there = mine_ref[:rows, :].astype(F32), more_ref[:rows, :].astype(F32)
        x = x + coeff[1] * jnp.where(ahead, here, there) + coeff[2] * jnp.where(ahead, there, here)
        x = x + coeff[3] * last_ref[:rows, :].astype(F32)
        blocks.append(x)
    first = slots_last(order_ref, slots)
    second = from_kept_twice()
    per = rows // HALF
    for c in range(4):
        x = jnp.concatenate(
            [blocks[k // per][HALF * (k % per) + 8 * c : HALF * (k % per) + 8 * c + 8] for k in range(slots)],
            axis=0,
        )
        x = jnp.dot(first, jnp.concatenate(split(x), axis=1), preferred_element_type=F32).astype(BF16)
        x = jnp.dot(x, second, preferred_element_type=F32)
        for i in range(8):
            out_ref[:, (8 * c + i) * LANES : (8 * c + i + 1) * LANES] = x[i * slots : (i + 1) * slots]


def paired(start_vector, extents, offsets, env_left, env_right, channel_mask):
    nodes = lax.axis_size("sector")
    ops = lax.axis_size("op")
    slots = start_vector.shape[0]
    cap = slots // nodes
    count = float(slots * nodes * B * B)
    swap_core = [(i, i ^ 1) for i in range(ops)]
    swap_x = [(i, i ^ 2) for i in range(ops)]
    left = jnp.transpose(env_left, (1, 0, 2))
    right = jnp.transpose(env_right, (1, 0, 2))
    meta = jnp.concatenate([offsets[None], jnp.transpose(extents), jnp.transpose(channel_mask)], axis=0)

    def route(t, back):
        pairs = []
        for h in range(nodes):
            for q in range(ops):
                to = (h + 2 * (q % 2) + t) % nodes
                a, b = h * ops + q, to * ops + q
                pairs.append((b, a) if back else (a, b))
        return pairs

    def across(x):
        return lax.ppermute(x, "op", swap_core)

    def shape(dims, dtype=F32):
        return jax.ShapeDtypeStruct(dims, dtype)

    environment = shape((cap, B, WIDE), BF16)
    vector = shape((cap, HALF, LANES))
    tile = shape((8, LANES))
    code = shape((cap * HALF + 16, LANES), jnp.int16)
    payload = shape((cap * HALF + 32, LANES), BF16)
    order, *ships, home = call(
        ship_kernel, "ship",
        (shape((slots,), jnp.int32), payload, payload, shape((slots * HALF, LANES), BF16)),
        (meta, start_vector), "sv", [pltpu.SMEM((nodes,), jnp.int32)], "svvv", 2.0, ROOMY, True)
    ships = [lax.ppermute(x, ("sector", "op"), route(t, False)) for t, x in enumerate(ships)]

    def arrange(env, *more):
        sets = call(
            arrange_kernel, "arrange", (environment,) * 4, (order, meta, env, *more), "ssv" + "v" * len(more),
            cost=3.0, limit=ARRANGE, compute=True)
        return sets[:2], [across(x) for x in sets[2:]]

    keep_left, got_left = arrange(left)
    ships = call(arrived_kernel, "arrived", (payload, payload), (*ships, keep_left[0]), "vva", cost=0.3)
    keep_right, got_right = arrange(right, *ships)
    envs = [(keep_left[t], keep_right[t], got_left[t], got_right[t]) for t in range(2)]

    def step(k):
        return lambda *refs: step_kernel(k, *refs)

    inner = [pltpu.VMEM((cap, LANES, 2 * WIDE), BF16)]
    basis = [[], []]
    along = [[], []]
    images = [None, None]
    early = []
    for t in range(2):
        q, y, scale = call(
            lambda *refs, t=t: start_kernel(count, nodes, t, *refs), "first", (vector, code, tile),
            (*ships, *envs[t]), "v" * 6, inner)
        basis[t].append(q)
        images[t] = (y, lax.ppermute(y, "op", swap_x))
    for k in range(1, ITERS):
        for t in range(2):
            outs = [vector, code, tile]
            if k == ITERS - 1:
                outs.append(shape(code.shape, BF16))
            q, y, a, *parcel = call(
                step(k), ("second", "third")[k - 1], tuple(outs),
                (ships[t], *images[t], *basis[t], *envs[t]), "v" * (7 + k), inner)
            basis[t].append(q)
            along[t].append(a)
            images[t] = (y, lax.ppermute(y, "op", swap_x))
            early += [lax.ppermute(x, ("sector", "op"), route(t, True)) for x in parcel]
    early = [(x, lax.ppermute(x, "op", swap_x)) for x in early]
    early += [tuple(across(x) for x in pair) for pair in early]
    early = [x for pair in early for x in pair]

    operands = []
    for t in range(2):
        operands += [ships[t], *images[t], *basis[t], *along[t]]
    *last, table = call(table_kernel, "table", (vector, vector, tile), operands, "v" * 16, cost=1.0)
    parcel = shape((cap * HALF + 16, LANES), BF16)
    late = call(
        pack_kernel, "pack", (parcel, parcel), (table, across(table), *last), "vvvv", cost=0.7)
    late = [lax.ppermute(x, ("sector", "op"), route(t, True)) for t, x in enumerate(late)]
    late += [across(x) for x in late]

    def finish(*refs):
        finish_kernel(count, nodes, *refs)

    return call(
        finish, "finish", (shape((slots, B * B)), shape((ITERS, ITERS))),
        (order, scale, home, *early, *late), "s" + "v" * 14)


def pack_rows(data, index, nodes, cap):
    slots = data.shape[0]
    hit = jnp.arange(nodes * cap, dtype=jnp.int32)[:, None] == index[None, :]
    source = jnp.sum(jnp.where(hit, jnp.arange(slots, dtype=jnp.int32)[None, :], 0), axis=1)
    filled = jnp.any(hit, axis=1)
    rows = jnp.take(data, source, axis=0)
    rows = jnp.where(filled[:, None], rows, jnp.zeros_like(rows))
    return rows.reshape(nodes, cap, data.shape[1])


def unpack_rows(arrived, index):
    flat = arrived.reshape(arrived.shape[0] * arrived.shape[1], arrived.shape[2])
    return jnp.take(flat, index, axis=0)


def general(start_vector, extents, offsets, env_left, env_right, channel_mask):
    nodes = lax.axis_size("sector")
    here_index = lax.axis_index("sector")
    slots = start_vector.shape[0]
    cap = max(1, slots // nodes)
    chans = env_left.shape[1]
    count = float(slots * nodes * B * B)
    slot_ids = jnp.arange(slots, dtype=jnp.int32)
    same = offsets[:, None] == offsets[None, :]
    earlier = slot_ids[None, :] < slot_ids[:, None]
    rank = jnp.sum((same & earlier).astype(jnp.int32), axis=1)
    send_index = (here_index + offsets) % nodes * cap + rank
    recv_index = (here_index - offsets) % nodes * cap + rank
    position = jnp.arange(B * B, dtype=jnp.int32)
    inside = ((position // B)[None, :] < extents[:, 0:1]) & (
        (position % B)[None, :] < extents[:, 1:2]
    )
    mask = inside.astype(jnp.float32)
    left = env_left.reshape(slots, chans, B, B)
    right_wide = env_right.reshape(slots, chans, B, B).astype(jnp.float32)
    chan = channel_mask.astype(jnp.float32)

    def squares(vector):
        return lax.psum(jnp.sum(vector * vector), "sector") / count

    def correlation_table(basis, image):
        local = [jnp.sum(vector * image) for vector in basis]
        local = local + [jnp.zeros((), jnp.float32)] * (ITERS - len(basis))
        return lax.psum(jnp.stack(local), "sector") / count

    masked = mask * start_vector.astype(jnp.float32)
    basis = [masked / jnp.sqrt(squares(masked) + 1e-06)]
    projections = jnp.zeros((ITERS, ITERS), jnp.float32)
    residual = masked
    for step in range(ITERS):
        moving = pack_rows(basis[step].astype(jnp.bfloat16), send_index, nodes, cap)
        arrived = lax.all_to_all(moving, "sector", split_axis=0, concat_axis=0, tiled=True)
        blocks = unpack_rows(arrived, recv_index).reshape(slots, B, B)
        inner = jnp.einsum("swab,sbc->swac", left, blocks, preferred_element_type=jnp.float32)
        inner = inner * chan[:, :, None, None]
        partial_image = jnp.einsum(
            "swac,swdc->sad", inner, right_wide, precision=lax.Precision.HIGHEST
        )
        total = lax.psum(partial_image.reshape(slots, B * B), "op")
        going = pack_rows(total, recv_index, nodes, cap)
        returned = lax.all_to_all(going, "sector", split_axis=0, concat_axis=0, tiled=True)
        apply_image = unpack_rows(returned, send_index)
        image = apply_image * mask
        coeffs = correlation_table(basis, image)
        residual = image
        for index in range(step + 1):
            projections = projections.at[index, step].set(coeffs[index])
            residual = residual - coeffs[index] * basis[index]
        if step + 1 < ITERS:
            basis.append(residual / jnp.sqrt(squares(residual) + 1e-06))
    return (residual, projections)


def solution(mesh):
    def on_device(start_vector, extents, offsets, env_left, env_right, channel_mask):
        nodes, ops = mesh.shape["sector"], mesh.shape["op"]
        slots, chans = env_left.shape[:2]
        fits = nodes == 4 and ops == 4 and slots == 8 * nodes and chans < 8
        body = paired if fits else general
        return body(start_vector, extents, offsets, env_left, env_right, channel_mask)

    return jax.shard_map(
        on_device,
        mesh=mesh,
        in_specs=(
            P(("groups", "sector"), None),
            P(("groups", "sector"), None),
            P("groups"),
            P(("groups", "sector"), "op", None),
            P(("groups", "sector"), "op", None),
            P(("groups", "sector"), "op"),
        ),
        out_specs=(P(("groups", "sector"), None), P("groups", None)),
        check_vma=False,
    )
```

```python
import jax
import jax.numpy as jnp
from jax import lax
from jax.experimental import pallas as pl
from jax.experimental.pallas import tpu as pltpu
from jax.sharding import PartitionSpec as P

B = 64
ITERS = 3
HALF = 32
LANES = 128
WIDE = 4 * LANES
F32 = jnp.float32
BF16 = jnp.bfloat16
VMEM_LIMIT = 24 * 1024 * 1024
ROOMY = 32 * 1024 * 1024
ARRANGE = 32 * 1024 * 1024


def position():
    return lax.axis_index("sector"), lax.axis_index("op") % 2


def iota(shape, dim):
    return lax.broadcasted_iota(jnp.int32, shape, dim)


def one_hot(condition):
    return jnp.where(condition, 1.0, 0.0).astype(BF16)


def kept_column(c):
    return (c % 2) * HALF + c // 2


def to_kept():
    row, col = iota((LANES, LANES), 0), iota((LANES, LANES), 1)
    return one_hot(row // B * B + kept_column(row % B) == col)


def from_kept_twice():
    row, col = iota((2 * LANES, LANES), 0) % LANES, iota((2 * LANES, LANES), 1)
    return one_hot(col // B * B + kept_column(col % B) == row)


def pair_to_kept():
    row, col = iota((2 * LANES, 2 * LANES), 0), iota((2 * LANES, 2 * LANES), 1)
    w, p, c = row // LANES, row // B % 2, row % B
    return one_hot(p * LANES + w * B + kept_column(c) == col)


def blocks_first(order_ref, base, count, slots):
    col, row = iota((8, 8 * slots), 1), iota((8, 8 * slots), 0)
    same = col // slots == row
    slot = col % slots
    parts = [
        jnp.where(same & (slot == order_ref[base + k]), 1.0, 0.0) for k in range(count)
    ]
    return jnp.concatenate(parts, axis=0).astype(BF16)


def slots_last(order_ref, slots):
    n = 8 * slots
    place = iota((1, n), 1) // 8
    slot = jnp.zeros((1, n), jnp.int32)
    for k in range(slots):
        slot = jnp.where(place == k, order_ref[k], slot)
    row, col = iota((n, n), 0), iota((n, n), 1)
    return one_hot((row // slots == col % 8) & (row % slots == slot))


def inside(rows, cols):
    lane = iota((HALF, LANES), 1)
    a = 2 * iota((HALF, LANES), 0) + lane // B
    kept = lane % B
    c = 2 * (kept % HALF) + kept // HALF
    return jnp.where((a.astype(F32) < rows) & (c.astype(F32) < cols), 1.0, 0.0)


def total_of(x):
    return jnp.sum(jnp.sum(x, axis=0, keepdims=True), axis=1, keepdims=True)


def wide(x):
    return jnp.broadcast_to(x, (1, LANES))


def split(x):
    high = x.astype(BF16)
    return high, (x - high.astype(F32)).astype(BF16)


def split_three(x):
    high, _ = split(x)
    rest = x - high.astype(F32)
    middle, low = split(rest)
    return high, middle, low


def call(kernel, name, out_shape, operands, kinds, scratch=(), out_kinds=None, cost=2.0, limit=VMEM_LIMIT,
         compute=False):
    space = {"s": pltpu.SMEM, "v": pltpu.VMEM, "h": pltpu.HBM, "a": pl.ANY}
    out_kinds = out_kinds or "v" * len(out_shape)
    return pl.pallas_call(
        kernel,
        out_shape=out_shape,
        in_specs=[pl.BlockSpec(memory_space=space[k]) for k in kinds],
        out_specs=tuple(pl.BlockSpec(memory_space=space[k]) for k in out_kinds),
        scratch_shapes=list(scratch),
        compiler_params=pltpu.CompilerParams(vmem_limit_bytes=limit),
        cost_estimate=pl.CostEstimate(
            flops=int(cost * 1.0e9) if compute else 0,
            bytes_accessed=1024 if compute else int(cost * 3.0e6),
            transcendentals=0,
        ),
        name=name,
    )(*operands)


def sort_slots(core, meta_ref, order_ref, seen):
    slots = order_ref.shape[0]
    nodes = seen.shape[0]
    cap = slots // nodes
    for o in range(nodes):
        seen[o] = 0
    for j in range(slots):
        o = meta_ref[0, j]
        rank = seen[o]
        seen[o] = rank + 1
        place = o * cap + rank + core * (slots // 2)
        order_ref[jnp.where(place >= slots, place - slots, place)] = j


def note(ref):
    return ref[ref.shape[0] - 32 :, :].astype(F32)


def arrived_kernel(near_in_ref, far_in_ref, _, near_ref, far_ref):
    near_ref[...] = near_in_ref[...]
    far_ref[...] = far_in_ref[...]


def riding_sums(ships):
    pieces = [note(ref)[16:19] for ref in ships]
    tile = jnp.concatenate(pieces + [jnp.zeros((HALF - 6, LANES), F32)], axis=0)
    tile = jnp.where(iota((HALF, LANES), 1) >= B, tile, 0.0)
    return jnp.concatenate([tile, jnp.zeros_like(tile)], axis=1)


def arrange_kernel(masked, *refs):
    ins, outs = refs[:-4], refs[-4:]
    if masked:
        first_ref, env_ref, meta_ref = ins
    else:
        first_ref, env_ref, *ships = ins
        riding = riding_sums(ships)
    chans, slots = env_ref.shape[:2]
    cap = outs[0].shape[0]
    first = first_ref[...]
    second = pair_to_kept()
    if masked:
        rows = []
        for w in range(8):
            row = meta_ref[3 + w : 4 + w, :].astype(F32) if w < chans else jnp.zeros((1, slots), F32)
            rows.append(jnp.broadcast_to(jnp.concatenate([row] * 8, axis=1), (LANES, 8 * slots)))
        mask = lax.dot_general(
            first, jnp.concatenate(rows, axis=0).astype(BF16), (((1,), (1,)), ((), ())),
            preferred_element_type=F32)
    blank = jnp.zeros((slots, LANES), BF16)
    for g in range(4):
        used = [w for w in (2 * g, 2 * g + 1) if w < chans]
        chunks = []
        for c in range(4):
            rows = []
            for i in range(8 * c, 8 * c + 8):
                parts = [env_ref[w, :, i * LANES : (i + 1) * LANES] for w in used]
                rows.append(jnp.concatenate(parts + [blank] * (2 - len(used)), axis=1))
            x = jnp.concatenate(rows, axis=0)
            x = jnp.dot(first, x, preferred_element_type=F32)
            if masked:
                x = x * mask[:, 2 * g * LANES : 2 * (g + 1) * LANES]
            chunks.append(jnp.dot(x.astype(BF16), second, preferred_element_type=F32))
        for k in range(slots):
            x = jnp.concatenate([chunk[8 * k : 8 * k + 8] for chunk in chunks], axis=0)
            if not masked and g == 3 and k in (2 * cap, 3 * cap):
                x = x + riding
            x = x.astype(BF16)
            for p in range(2):
                outs[k // cap][k % cap, p * HALF : (p + 1) * HALF, g * LANES : (g + 1) * LANES] = x[
                    :, p * LANES : (p + 1) * LANES
                ]


def ship_kernel(meta_ref, start_ref, first_ref, last_ref, near_ref, far_ref, home_ref, order_ref, seen):
    sort_slots(position()[1], meta_ref, order_ref, seen)
    slots = start_ref.shape[0]
    cap = slots // 4
    first = blocks_first(order_ref, 0, slots, slots)
    first_ref[...] = first
    last_ref[...] = slots_last(order_ref, slots)
    second = to_kept()
    chunks = []
    for c in range(4):
        rows = [start_ref[:, i * LANES : (i + 1) * LANES] for i in range(8 * c, 8 * c + 8)]
        x = jnp.dot(first, jnp.concatenate(rows, axis=0), preferred_element_type=F32).astype(BF16)
        chunks.append(jnp.dot(x, second, preferred_element_type=F32))
    halves = []
    for k in range(slots):
        slot = order_ref[k]
        x = jnp.concatenate([chunk[8 * k : 8 * k + 8] for chunk in chunks], axis=0)
        x = x * inside(meta_ref[1, slot].astype(F32), meta_ref[2, slot].astype(F32))
        home_ref[HALF * k : HALF * (k + 1), :] = x.astype(BF16)
        if k < 2 * cap:
            (near_ref, far_ref)[k // cap][HALF * (k % cap) : HALF * (k % cap + 1), :] = x.astype(BF16)
        if k % (2 * cap) == 0:
            halves.append(x * x)
        else:
            halves[-1] = halves[-1] + x * x
    squares = wide(total_of(halves[0]) + total_of(halves[1]))
    pieces = [v.astype(F32) for v in split_three(squares)]
    blank = jnp.zeros((2 * 16 - 2 * cap - 3, LANES), F32)
    for t, ref in enumerate((near_ref, far_ref)):
        lines = []
        for d in range(2):
            for k in range(cap):
                lines.append(jnp.full((1, LANES), meta_ref[1 + d, order_ref[t * cap + k]].astype(F32)))
        ref[HALF * cap :, :] = jnp.concatenate(lines + pieces + [blank], axis=0).astype(BF16)


BITS = 14


def encode(s, x, out_ref):
    largest = jnp.max(jnp.max(jnp.abs(x), axis=0, keepdims=True), axis=1, keepdims=True)
    power = wide(jnp.ceil(jnp.log2(jnp.maximum(largest, 1e-30))))
    code = jnp.floor(x * jnp.exp2(BITS - power) + 0.5)
    out_ref[HALF * s : HALF * (s + 1), :] = code.astype(jnp.int32).astype(jnp.int16)
    return power


def encode_end(powers, out_ref):
    cap = len(powers)
    tail = jnp.concatenate(powers + [jnp.zeros((16 - cap, LANES), F32)], axis=0)
    out_ref[HALF * cap :, :] = tail.astype(jnp.int32).astype(jnp.int16)


def decode(ref, s, scales):
    return ref[HALF * s : HALF * (s + 1), :].astype(jnp.int32).astype(F32) * scales[s : s + 1]


def decode_scales(ref):
    return jnp.exp2(ref[ref.shape[0] - 16 :, :].astype(jnp.int32).astype(F32) - BITS)


def block_diagonal(x):
    low = iota((HALF, LANES), 1) < B
    swapped = pltpu.roll(x, B, 1)
    zero = jnp.zeros_like(x)
    two = jnp.concatenate(
        [
            jnp.where(low, x, zero),
            jnp.where(low, swapped, zero),
            jnp.where(low, zero, swapped),
            jnp.where(low, zero, x),
        ],
        axis=0,
    )
    blank = jnp.zeros_like(two)
    return jnp.concatenate(
        [jnp.concatenate([two, blank], axis=1), jnp.concatenate([blank, two], axis=1)], axis=0
    )


def product(q_ref, envs, y_ref, inner_ref, rounded):
    count = q_ref.shape[0]
    span = 2 * LANES
    keep_left, keep_right, got_left, got_right = envs
    for s in range(count):
        high, low = split(block_diagonal(q_ref[s]))
        left = jnp.concatenate(
            [ref[s, :, g * span : (g + 1) * span] for ref in (keep_left, got_left) for g in range(2)], axis=0
        )
        inner = jnp.dot(left, high, preferred_element_type=F32)
        if not rounded:
            inner = inner + jnp.dot(left, low, preferred_element_type=F32)
        high, low = split(inner)
        for k in range(4):
            inner_ref[s, :B, k * span : (k + 1) * span] = high[k * B : (k + 1) * B]
            inner_ref[s, B:, k * span : (k + 1) * span] = low[k * B : (k + 1) * B]
    powers = []
    for s in range(count):
        right = jnp.concatenate([keep_right[s], got_right[s]], axis=1)
        both = lax.dot_general(inner_ref[s], right, (((1,), (1,)), ((), ())), preferred_element_type=F32)
        image = both[:B] + both[B:]
        powers.append(encode(s, jnp.concatenate([image[:HALF], image[HALF:]], axis=1), y_ref))
    encode_end(powers, y_ref)


def start_kernel(count, nodes, t, *refs):
    ships, envs, (q_ref, y_ref, scale_ref, inner_ref) = refs[:2], refs[2:6], refs[6:]
    node, core = position()
    ship_ref = ships[t]
    mine = [note(ref)[16:19] for ref in ships]
    tile = envs[3][0, :HALF, WIDE - LANES :].astype(F32)
    tile = jnp.where(iota((HALF, LANES), 1) >= B, tile, pltpu.roll(tile, B, 1))
    theirs = [tile[0:3], tile[3:6]]
    by_node = []
    for e in range(nodes):
        value = jnp.zeros((1, LANES), F32)
        for sums, c in ((mine, core), (theirs, 1 - core)):
            for hop, p in enumerate(sums):
                source = lax.rem(node + 2 * nodes - 2 * c - hop, nodes)
                value = value + jnp.where(source == e, p[0:1] + p[1:2] + p[2:3], 0.0)
        by_node.append(value)
    squares = (by_node[0] + by_node[1]) + (by_node[2] + by_node[3])
    scale = 1.0 / jnp.sqrt(squares / count + 1e-06)
    scale_ref[...] = jnp.broadcast_to(scale, scale_ref.shape)
    for s in range(q_ref.shape[0]):
        q_ref[s] = ship_ref[HALF * s : HALF * (s + 1), :].astype(F32) * scale
    product(q_ref, envs, y_ref, inner_ref, True)


def orthogonal(ship_ref, own_ref, other_ref, basis, q_ref):
    n = note(ship_ref)
    cap = q_ref.shape[0]
    ahead = lax.axis_index("op") < 2
    own_scales, other_scales = decode_scales(own_ref), decode_scales(other_ref)
    for s in range(cap):
        own, other = decode(own_ref, s, own_scales), decode(other_ref, s, other_scales)
        image = jnp.where(ahead, own, other) + jnp.where(ahead, other, own)
        q_ref[s] = image * inside(n[s : s + 1], n[cap + s : cap + s + 1])
    image = q_ref[...].reshape(cap * HALF, LANES)
    rows = []
    rest = image
    for ref in basis:
        q = ref[...].reshape(cap * HALF, LANES)
        length = total_of(q * q)
        along = total_of(q * image)
        row = wide(jnp.where(length > 0, along / jnp.where(length > 0, length, 1.0), 0.0))
        rest = rest - row * q
        rows.append(row)
    q_ref[...] = rest.reshape(q_ref.shape)
    return rows


def step_kernel(count, *refs):
    ship_ref, own_ref, other_ref = refs[:3]
    basis = refs[3 : 3 + count]
    envs = refs[3 + count : 7 + count]
    q_ref, y_ref, along_ref, *parcel_ref, inner_ref = refs[7 + count :]
    rows = orthogonal(ship_ref, own_ref, other_ref, basis, q_ref)
    along_ref[...] = jnp.concatenate(rows + [jnp.zeros((8 - count, LANES), F32)], axis=0)
    for ref in parcel_ref:
        mine = jnp.where(lax.axis_index("op") < 2, basis[1][...], q_ref[...])
        mine = mine.reshape(-1, LANES).astype(BF16)
        blank = jnp.zeros((ref.shape[0] - mine.shape[0], LANES), BF16)
        ref[...] = jnp.concatenate([mine, blank], axis=0)
    product(q_ref, envs, y_ref, inner_ref, False)


def line_of(values):
    lane = iota((1, LANES), 1)
    line = jnp.zeros((1, LANES), F32)
    for k, value in enumerate(values):
        line = jnp.where(lane == k, value, line)
    return line


def table_kernel(*refs):
    out_refs, table_ref = refs[16:18], refs[18]
    lines = []
    for t in range(2):
        ship_ref, own_ref, other_ref, q0, q1, q2, c1, c2 = refs[8 * t : 8 * t + 8]
        last = orthogonal(ship_ref, own_ref, other_ref, (q0, q1, q2), out_refs[t])
        vectors = [ref[...].reshape(-1, LANES) for ref in (q0, q1, q2, out_refs[t])]
        values = [total_of(vectors[i] * vectors[j]) for i in range(4) for j in range(i, 4)]
        lines.append(line_of(values + [c1[0:1], c2[0:1], c2[1:2]] + last))
    table_ref[...] = jnp.concatenate(lines + [jnp.zeros((6, LANES), F32)], axis=0)


def pack_kernel(table_ref, other_ref, *refs):
    core = position()[1]
    mine, other = table_ref[0:2, :], other_ref[0:2, :]
    lines = jnp.concatenate([jnp.where(core == 0, mine, other), jnp.where(core == 0, other, mine)], axis=0)
    pieces = [v.astype(F32) for v in split_three(lines)]
    tail = jnp.concatenate(pieces + [jnp.zeros((4, LANES), F32)], axis=0).astype(BF16)
    for ref, out_ref in zip(refs[:2], refs[2:]):
        rows = ref.shape[0] * HALF
        out_ref[:rows, :] = ref[...].reshape(rows, LANES).astype(BF16)
        out_ref[rows:, :] = tail


def combine(count, take):
    gram = {}
    row = 0
    for i in range(4):
        for j in range(i, 4):
            gram[i, j] = gram[j, i] = take(row)
            row += 1
    one = jnp.ones_like(gram[0, 0])
    images = [
        [take(10), one, None, None],
        [take(11), take(12), one, None],
        [take(13), take(14), take(15), one],
    ]

    def mean(u, v):
        acc = None
        for i in range(4):
            for j in range(4):
                if u[i] is not None and v[j] is not None:
                    term = u[i] * v[j] * gram[i, j]
                    acc = term if acc is None else acc + term
        return jnp.sum(acc, axis=0, keepdims=True) / count

    basis = [[one, None, None, None]]
    projections = {}
    for k in range(ITERS):
        image = [None] * 4
        for z, parts in zip(basis[k], images):
            for m, v in enumerate(parts):
                if z is not None and v is not None:
                    image[m] = z * v if image[m] is None else image[m] + z * v
        rest = list(image)
        for i in range(k + 1):
            p = mean(basis[i], image)
            projections[i, k] = p
            for m, v in enumerate(basis[i]):
                if v is not None:
                    rest[m] = rest[m] - p * v
        if k + 1 < ITERS:
            scale = 1.0 / jnp.sqrt(mean(rest, rest) + 1e-06)
            basis.append([None if v is None else v * scale for v in rest])
    return projections, rest


def finish_kernel(count, nodes, back_ref, scale_ref, home_ref, *refs):
    early, late, (out_ref, proj_ref) = refs[:8], refs[8:12], refs[12:]
    node, core = position()
    slots = out_ref.shape[0]
    rows = home_ref.shape[0] // 4
    sources = []
    lines = [jnp.zeros((4, LANES), F32) for _ in range(nodes)]
    for k, ref in enumerate(late):
        hop = 2 * (core if k < 2 else 1 - core) + k % 2
        host = lax.rem(node + hop, nodes)
        tail = ref[rows:, :].astype(F32)
        four = tail[0:4] + tail[4:8] + tail[8:12]
        lines = [jnp.where(host == e, four, v) for e, v in enumerate(lines)]
        sources.append((*early[2 * k : 2 * k + 2], ref, host * 4 + hop))
    table = jnp.concatenate(lines, axis=0)
    sets = 4 * nodes
    projections, rest = combine(
        count, lambda k: jnp.broadcast_to(table[:, k : k + 1], (sets, LANES)))
    lines = [line_of([projections.get((i, k), 0.0) for k in range(ITERS)]) for i in range(ITERS)]
    proj_ref[...] = jnp.concatenate(lines, axis=0)[:, :ITERS]
    scale = scale_ref[0:1, :]
    blocks = []
    ahead = lax.axis_index("op") < 2
    for k, (mine_ref, more_ref, last_ref, index) in enumerate(sources):
        mine = iota((sets, LANES), 0) == index
        coeff = [jnp.sum(jnp.where(mine, v, 0.0), axis=0, keepdims=True) for v in rest]
        x = coeff[0] * (home_ref[rows * k : rows * (k + 1), :].astype(F32) * scale)
        here, there = mine_ref[:rows, :].astype(F32), more_ref[:rows, :].astype(F32)
        x = x + coeff[1] * jnp.where(ahead, here, there) + coeff[2] * jnp.where(ahead, there, here)
        x = x + coeff[3] * last_ref[:rows, :].astype(F32)
        blocks.append(x)
    first = back_ref[...]
    second = from_kept_twice()
    per = rows // HALF
    for c in range(4):
        x = jnp.concatenate(
            [blocks[k // per][HALF * (k % per) + 8 * c : HALF * (k % per) + 8 * c + 8] for k in range(slots)],
            axis=0,
        )
        x = jnp.dot(first, jnp.concatenate(split(x), axis=1), preferred_element_type=F32).astype(BF16)
        x = jnp.dot(x, second, preferred_element_type=F32)
        for i in range(8):
            out_ref[:, (8 * c + i) * LANES : (8 * c + i + 1) * LANES] = x[i * slots : (i + 1) * slots]


def paired(start_vector, extents, offsets, env_left, env_right, channel_mask):
    nodes = lax.axis_size("sector")
    ops = lax.axis_size("op")
    slots = start_vector.shape[0]
    cap = slots // nodes
    count = float(slots * nodes * B * B)
    swap_core = [(i, i ^ 1) for i in range(ops)]
    swap_x = [(i, i ^ 2) for i in range(ops)]
    left = jnp.transpose(env_left, (1, 0, 2))
    right = jnp.transpose(env_right, (1, 0, 2))
    meta = jnp.concatenate([offsets[None], jnp.transpose(extents), jnp.transpose(channel_mask)], axis=0)

    def route(t, back):
        pairs = []
        for h in range(nodes):
            for q in range(ops):
                to = (h + 2 * (q % 2) + t) % nodes
                a, b = h * ops + q, to * ops + q
                pairs.append((b, a) if back else (a, b))
        return pairs

    def across(x):
        return lax.ppermute(x, "op", swap_core)

    def shape(dims, dtype=F32):
        return jax.ShapeDtypeStruct(dims, dtype)

    environment = shape((cap, B, WIDE), BF16)
    vector = shape((cap, HALF, LANES))
    tile = shape((8, LANES))
    code = shape((cap * HALF + 16, LANES), jnp.int16)
    payload = shape((cap * HALF + 32, LANES), BF16)
    one_hots = shape((8 * slots, 8 * slots), BF16)
    first, back, *ships, home = call(
        ship_kernel, "ship",
        (one_hots, one_hots, payload, payload, shape((slots * HALF, LANES), BF16)),
        (meta, start_vector), "sv",
        [pltpu.SMEM((slots,), jnp.int32), pltpu.SMEM((nodes,), jnp.int32)], "vvvvv", 2.0, ROOMY, True)
    ships = [lax.ppermute(x, ("sector", "op"), route(t, False)) for t, x in enumerate(ships)]

    def arrange(masked, operands, kinds):
        sets = call(
            lambda *refs: arrange_kernel(masked, *refs), "arrange", (environment,) * 4, operands, kinds,
            cost=3.0, limit=ARRANGE, compute=True)
        return sets[:2], [across(x) for x in sets[2:]]

    keep_left, got_left = arrange(True, (first, left, meta), "vvv")
    ships = call(arrived_kernel, "arrived", (payload, payload), (*ships, keep_left[0]), "vva", cost=0.3)
    keep_right, got_right = arrange(False, (first, right, *ships), "vvvv")
    envs = [(keep_left[t], keep_right[t], got_left[t], got_right[t]) for t in range(2)]

    def step(k):
        return lambda *refs: step_kernel(k, *refs)

    inner = [pltpu.VMEM((cap, LANES, 2 * WIDE), BF16)]
    basis = [[], []]
    along = [[], []]
    images = [None, None]
    early = []
    for t in range(2):
        q, y, scale = call(
            lambda *refs, t=t: start_kernel(count, nodes, t, *refs), "first", (vector, code, tile),
            (*ships, *envs[t]), "v" * 6, inner)
        basis[t].append(q)
        images[t] = (y, lax.ppermute(y, "op", swap_x))
    for k in range(1, ITERS):
        for t in range(2):
            outs = [vector, code, tile]
            if k == ITERS - 1:
                outs.append(shape(code.shape, BF16))
            q, y, a, *parcel = call(
                step(k), ("second", "third")[k - 1], tuple(outs),
                (ships[t], *images[t], *basis[t], *envs[t]), "v" * (7 + k), inner)
            basis[t].append(q)
            along[t].append(a)
            images[t] = (y, lax.ppermute(y, "op", swap_x))
            early += [lax.ppermute(x, ("sector", "op"), route(t, True)) for x in parcel]
    early = [(x, lax.ppermute(x, "op", swap_x)) for x in early]
    early += [tuple(across(x) for x in pair) for pair in early]
    early = [x for pair in early for x in pair]

    operands = []
    for t in range(2):
        operands += [ships[t], *images[t], *basis[t], *along[t]]
    *last, table = call(table_kernel, "table", (vector, vector, tile), operands, "v" * 16, cost=1.0)
    parcel = shape((cap * HALF + 16, LANES), BF16)
    late = call(
        pack_kernel, "pack", (parcel, parcel), (table, across(table), *last), "vvvv", cost=0.7)
    late = [lax.ppermute(x, ("sector", "op"), route(t, True)) for t, x in enumerate(late)]
    late += [across(x) for x in late]

    def finish(*refs):
        finish_kernel(count, nodes, *refs)

    return call(
        finish, "finish", (shape((slots, B * B)), shape((ITERS, ITERS))),
        (back, scale, home, *early, *late), "v" * 15)


def pack_rows(data, index, nodes, cap):
    slots = data.shape[0]
    hit = jnp.arange(nodes * cap, dtype=jnp.int32)[:, None] == index[None, :]
    source = jnp.sum(jnp.where(hit, jnp.arange(slots, dtype=jnp.int32)[None, :], 0), axis=1)
    filled = jnp.any(hit, axis=1)
    rows = jnp.take(data, source, axis=0)
    rows = jnp.where(filled[:, None], rows, jnp.zeros_like(rows))
    return rows.reshape(nodes, cap, data.shape[1])


def unpack_rows(arrived, index):
    flat = arrived.reshape(arrived.shape[0] * arrived.shape[1], arrived.shape[2])
    return jnp.take(flat, index, axis=0)


def general(start_vector, extents, offsets, env_left, env_right, channel_mask):
    nodes = lax.axis_size("sector")
    here_index = lax.axis_index("sector")
    slots = start_vector.shape[0]
    cap = max(1, slots // nodes)
    chans = env_left.shape[1]
    count = float(slots * nodes * B * B)
    slot_ids = jnp.arange(slots, dtype=jnp.int32)
    same = offsets[:, None] == offsets[None, :]
    earlier = slot_ids[None, :] < slot_ids[:, None]
    rank = jnp.sum((same & earlier).astype(jnp.int32), axis=1)
    send_index = (here_index + offsets) % nodes * cap + rank
    recv_index = (here_index - offsets) % nodes * cap + rank
    position = jnp.arange(B * B, dtype=jnp.int32)
    inside = ((position // B)[None, :] < extents[:, 0:1]) & (
        (position % B)[None, :] < extents[:, 1:2]
    )
    mask = inside.astype(jnp.float32)
    left = env_left.reshape(slots, chans, B, B)
    right_wide = env_right.reshape(slots, chans, B, B).astype(jnp.float32)
    chan = channel_mask.astype(jnp.float32)

    def squares(vector):
        return lax.psum(jnp.sum(vector * vector), "sector") / count

    def correlation_table(basis, image):
        local = [jnp.sum(vector * image) for vector in basis]
        local = local + [jnp.zeros((), jnp.float32)] * (ITERS - len(basis))
        return lax.psum(jnp.stack(local), "sector") / count

    masked = mask * start_vector.astype(jnp.float32)
    basis = [masked / jnp.sqrt(squares(masked) + 1e-06)]
    projections = jnp.zeros((ITERS, ITERS), jnp.float32)
    residual = masked
    for step in range(ITERS):
        moving = pack_rows(basis[step].astype(jnp.bfloat16), send_index, nodes, cap)
        arrived = lax.all_to_all(moving, "sector", split_axis=0, concat_axis=0, tiled=True)
        blocks = unpack_rows(arrived, recv_index).reshape(slots, B, B)
        inner = jnp.einsum("swab,sbc->swac", left, blocks, preferred_element_type=jnp.float32)
        inner = inner * chan[:, :, None, None]
        partial_image = jnp.einsum(
            "swac,swdc->sad", inner, right_wide, precision=lax.Precision.HIGHEST
        )
        total = lax.psum(partial_image.reshape(slots, B * B), "op")
        going = pack_rows(total, recv_index, nodes, cap)
        returned = lax.all_to_all(going, "sector", split_axis=0, concat_axis=0, tiled=True)
        apply_image = unpack_rows(returned, send_index)
        image = apply_image * mask
        coeffs = correlation_table(basis, image)
        residual = image
        for index in range(step + 1):
            projections = projections.at[index, step].set(coeffs[index])
            residual = residual - coeffs[index] * basis[index]
        if step + 1 < ITERS:
            basis.append(residual / jnp.sqrt(squares(residual) + 1e-06))
    return (residual, projections)


def solution(mesh):
    def on_device(start_vector, extents, offsets, env_left, env_right, channel_mask):
        nodes, ops = mesh.shape["sector"], mesh.shape["op"]
        slots, chans = env_left.shape[:2]
        fits = nodes == 4 and ops == 4 and slots == 8 * nodes and chans < 8
        body = paired if fits else general
        return body(start_vector, extents, offsets, env_left, env_right, channel_mask)

    return jax.shard_map(
        on_device,
        mesh=mesh,
        in_specs=(
            P(("groups", "sector"), None),
            P(("groups", "sector"), None),
            P("groups"),
            P(("groups", "sector"), "op", None),
            P(("groups", "sector"), "op", None),
            P(("groups", "sector"), "op"),
        ),
        out_specs=(P(("groups", "sector"), None), P("groups", None)),
        check_vma=False,
    )
```

```python
import jax
import jax.numpy as jnp
from jax import lax
from jax.experimental import pallas as pl
from jax.experimental.pallas import tpu as pltpu
from jax.sharding import PartitionSpec as P

B = 64
ITERS = 3
HALF = 32
LANES = 128
WIDE = 4 * LANES
F32 = jnp.float32
BF16 = jnp.bfloat16
VMEM_LIMIT = 24 * 1024 * 1024
ROOMY = 32 * 1024 * 1024
ARRANGE = 32 * 1024 * 1024


def position():
    return lax.axis_index("sector"), lax.axis_index("op") % 2


def iota(shape, dim):
    return lax.broadcasted_iota(jnp.int32, shape, dim)


def one_hot(condition):
    return jnp.where(condition, 1.0, 0.0).astype(BF16)


def kept_column(c):
    return (c % 2) * HALF + c // 2


def to_kept():
    row, col = iota((LANES, LANES), 0), iota((LANES, LANES), 1)
    return one_hot(row // B * B + kept_column(row % B) == col)


def from_kept_twice():
    row, col = iota((2 * LANES, LANES), 0) % LANES, iota((2 * LANES, LANES), 1)
    return one_hot(col // B * B + kept_column(col % B) == row)


def pair_to_kept():
    row, col = iota((2 * LANES, 2 * LANES), 0), iota((2 * LANES, 2 * LANES), 1)
    w, p, c = row // LANES, row // B % 2, row % B
    return one_hot(p * LANES + w * B + kept_column(c) == col)


def blocks_first(order_ref, base, count, slots):
    col, row = iota((8, 8 * slots), 1), iota((8, 8 * slots), 0)
    same = col // slots == row
    slot = col % slots
    parts = [
        jnp.where(same & (slot == order_ref[base + k]), 1.0, 0.0) for k in range(count)
    ]
    return jnp.concatenate(parts, axis=0).astype(BF16)


def spread(first, lines):
    rows = []
    for line in lines:
        row = jnp.concatenate([line.astype(F32)] * 8, axis=1)
        rows.append(jnp.broadcast_to(row, (LANES, row.shape[1])))
    return lax.dot_general(
        first, jnp.concatenate(rows, axis=0).astype(BF16), (((1,), (1,)), ((), ())),
        preferred_element_type=F32)


def slots_last(order_ref, slots):
    n = 8 * slots
    place = iota((1, n), 1) // 8
    slot = jnp.zeros((1, n), jnp.int32)
    for k in range(slots):
        slot = jnp.where(place == k, order_ref[k], slot)
    row, col = iota((n, n), 0), iota((n, n), 1)
    return one_hot((row // slots == col % 8) & (row % slots == slot))


def inside(rows, cols):
    lane = iota((HALF, LANES), 1)
    a = 2 * iota((HALF, LANES), 0) + lane // B
    kept = lane % B
    c = 2 * (kept % HALF) + kept // HALF
    return jnp.where((a.astype(F32) < rows) & (c.astype(F32) < cols), 1.0, 0.0)


def total_of(x):
    return jnp.sum(jnp.sum(x, axis=0, keepdims=True), axis=1, keepdims=True)


def wide(x):
    return jnp.broadcast_to(x, (1, LANES))


def split(x):
    high = x.astype(BF16)
    return high, (x - high.astype(F32)).astype(BF16)


def split_three(x):
    high, _ = split(x)
    rest = x - high.astype(F32)
    middle, low = split(rest)
    return high, middle, low


def call(kernel, name, out_shape, operands, kinds, scratch=(), out_kinds=None, cost=2.0, limit=VMEM_LIMIT,
         compute=False):
    space = {"s": pltpu.SMEM, "v": pltpu.VMEM, "h": pltpu.HBM, "a": pl.ANY}
    out_kinds = out_kinds or "v" * len(out_shape)
    return pl.pallas_call(
        kernel,
        out_shape=out_shape,
        in_specs=[pl.BlockSpec(memory_space=space[k]) for k in kinds],
        out_specs=tuple(pl.BlockSpec(memory_space=space[k]) for k in out_kinds),
        scratch_shapes=list(scratch),
        compiler_params=pltpu.CompilerParams(vmem_limit_bytes=limit),
        cost_estimate=pl.CostEstimate(
            flops=int(cost * 1.0e9) if compute else 0,
            bytes_accessed=1024 if compute else int(cost * 3.0e6),
            transcendentals=0,
        ),
        name=name,
    )(*operands)


def sort_slots(core, meta_ref, order_ref, seen):
    slots = order_ref.shape[0]
    nodes = seen.shape[0]
    cap = slots // nodes
    for o in range(nodes):
        seen[o] = 0
    for j in range(slots):
        o = meta_ref[0, j]
        rank = seen[o]
        seen[o] = rank + 1
        place = o * cap + rank + core * (slots // 2)
        order_ref[jnp.where(place >= slots, place - slots, place)] = j


def note(ref):
    return ref[ref.shape[0] - 32 :, :].astype(F32)


def arrived_kernel(near_in_ref, far_in_ref, _, near_ref, far_ref):
    near_ref[...] = near_in_ref[...]
    far_ref[...] = far_in_ref[...]


def riding_sums(ships):
    pieces = [note(ref)[16:19] for ref in ships]
    tile = jnp.concatenate(pieces + [jnp.zeros((HALF - 6, LANES), F32)], axis=0)
    tile = jnp.where(iota((HALF, LANES), 1) >= B, tile, 0.0)
    return jnp.concatenate([tile, jnp.zeros_like(tile)], axis=1)


def arrange_kernel(masked, *refs):
    ins, outs = refs[:-4], refs[-4:]
    if masked:
        first_ref, env_ref, meta_ref = ins
    else:
        first_ref, env_ref, *ships = ins
        riding = riding_sums(ships)
    chans, slots = env_ref.shape[:2]
    cap = outs[0].shape[0]
    first = first_ref[...]
    second = pair_to_kept()
    if masked:
        lines = [meta_ref[3 + w : 4 + w, :] for w in range(chans)]
        mask = spread(first, lines + [jnp.zeros_like(lines[0])] * (8 - chans))
    blank = jnp.zeros((slots, LANES), BF16)
    for g in range(4):
        used = [w for w in (2 * g, 2 * g + 1) if w < chans]
        chunks = []
        for c in range(4):
            rows = []
            for i in range(8 * c, 8 * c + 8):
                parts = [env_ref[w, :, i * LANES : (i + 1) * LANES] for w in used]
                rows.append(jnp.concatenate(parts + [blank] * (2 - len(used)), axis=1))
            x = jnp.concatenate(rows, axis=0)
            x = jnp.dot(first, x, preferred_element_type=F32)
            if masked:
                x = x * mask[:, 2 * g * LANES : 2 * (g + 1) * LANES]
            chunks.append(jnp.dot(x.astype(BF16), second, preferred_element_type=F32))
        for k in range(slots):
            x = jnp.concatenate([chunk[8 * k : 8 * k + 8] for chunk in chunks], axis=0)
            if not masked and g == 3 and k in (2 * cap, 3 * cap):
                x = x + riding
            x = x.astype(BF16)
            for p in range(2):
                outs[k // cap][k % cap, p * HALF : (p + 1) * HALF, g * LANES : (g + 1) * LANES] = x[
                    :, p * LANES : (p + 1) * LANES
                ]


def ship_kernel(meta_ref, table_ref, start_ref, first_ref, last_ref, near_ref, far_ref, home_ref, order_ref, seen):
    sort_slots(position()[1], meta_ref, order_ref, seen)
    slots = start_ref.shape[0]
    cap = slots // 4
    first = blocks_first(order_ref, 0, slots, slots)
    first_ref[...] = first
    last_ref[...] = slots_last(order_ref, slots)
    second = to_kept()
    bounds = spread(first, [table_ref[1 + d : 2 + d, :] for d in range(2)])
    tall, broad = bounds[:, :LANES], bounds[:, LANES:]
    lane, step = iota(tall.shape, 1), iota(tall.shape, 0) % 8
    kept = lane % B
    a = (2 * step + lane // B).astype(F32)
    columns = jnp.where((2 * (kept % HALF) + kept // HALF).astype(F32) < broad, 1.0, 0.0)
    chunks = []
    squares = None
    for c in range(4):
        rows = [start_ref[:, i * LANES : (i + 1) * LANES] for i in range(8 * c, 8 * c + 8)]
        x = jnp.dot(first, jnp.concatenate(rows, axis=0), preferred_element_type=F32).astype(BF16)
        x = jnp.dot(x, second, preferred_element_type=F32) * jnp.where(a + 16 * c < tall, columns, 0.0)
        chunks.append(x)
        squares = x * x if squares is None else squares + x * x
    for k in range(slots):
        x = jnp.concatenate([chunk[8 * k : 8 * k + 8] for chunk in chunks], axis=0).astype(BF16)
        home_ref[HALF * k : HALF * (k + 1), :] = x
        if k < 2 * cap:
            (near_ref, far_ref)[k // cap][HALF * (k % cap) : HALF * (k % cap + 1), :] = x
    half = squares.shape[0] // 2
    halves = [squares[:half], squares[half:]]
    squares = wide(total_of(halves[0]) + total_of(halves[1]))
    pieces = [v.astype(F32) for v in split_three(squares)]
    blank = jnp.zeros((2 * 16 - 2 * cap - 3, LANES), F32)
    for t, ref in enumerate((near_ref, far_ref)):
        lines = []
        for d in range(2):
            for k in range(cap):
                at = 8 * (t * cap + k)
                lines.append((tall, broad)[d][at : at + 1])
        ref[HALF * cap :, :] = jnp.concatenate(lines + pieces + [blank], axis=0).astype(BF16)


BITS = 14


def encode(s, x, out_ref):
    largest = jnp.max(jnp.max(jnp.abs(x), axis=0, keepdims=True), axis=1, keepdims=True)
    power = wide(jnp.ceil(jnp.log2(jnp.maximum(largest, 1e-30))))
    code = jnp.floor(x * jnp.exp2(BITS - power) + 0.5)
    out_ref[HALF * s : HALF * (s + 1), :] = code.astype(jnp.int32).astype(jnp.int16)
    return power


def encode_end(powers, out_ref):
    cap = len(powers)
    tail = jnp.concatenate(powers + [jnp.zeros((16 - cap, LANES), F32)], axis=0)
    out_ref[HALF * cap :, :] = tail.astype(jnp.int32).astype(jnp.int16)


def decode(ref, s, scales):
    return ref[HALF * s : HALF * (s + 1), :].astype(jnp.int32).astype(F32) * scales[s : s + 1]


def decode_scales(ref):
    return jnp.exp2(ref[ref.shape[0] - 16 :, :].astype(jnp.int32).astype(F32) - BITS)


def block_diagonal(x):
    low = iota((HALF, LANES), 1) < B
    swapped = pltpu.roll(x, B, 1)
    zero = jnp.zeros_like(x)
    two = jnp.concatenate(
        [
            jnp.where(low, x, zero),
            jnp.where(low, swapped, zero),
            jnp.where(low, zero, swapped),
            jnp.where(low, zero, x),
        ],
        axis=0,
    )
    blank = jnp.zeros_like(two)
    return jnp.concatenate(
        [jnp.concatenate([two, blank], axis=1), jnp.concatenate([blank, two], axis=1)], axis=0
    )


def product(q_ref, envs, y_ref, inner_ref, rounded):
    count = q_ref.shape[0]
    span = 2 * LANES
    keep_left, keep_right, got_left, got_right = envs
    for s in range(count):
        high, low = split(block_diagonal(q_ref[s]))
        left = jnp.concatenate(
            [ref[s, :, g * span : (g + 1) * span] for ref in (keep_left, got_left) for g in range(2)], axis=0
        )
        inner = jnp.dot(left, high, preferred_element_type=F32)
        if not rounded:
            inner = inner + jnp.dot(left, low, preferred_element_type=F32)
        high, low = split(inner)
        for k in range(4):
            inner_ref[s, :B, k * span : (k + 1) * span] = high[k * B : (k + 1) * B]
            inner_ref[s, B:, k * span : (k + 1) * span] = low[k * B : (k + 1) * B]
    powers = []
    for s in range(count):
        right = jnp.concatenate([keep_right[s], got_right[s]], axis=1)
        both = lax.dot_general(inner_ref[s], right, (((1,), (1,)), ((), ())), preferred_element_type=F32)
        image = both[:B] + both[B:]
        powers.append(encode(s, jnp.concatenate([image[:HALF], image[HALF:]], axis=1), y_ref))
    encode_end(powers, y_ref)


def start_kernel(count, nodes, t, *refs):
    ships, envs, (q_ref, y_ref, scale_ref, inner_ref) = refs[:2], refs[2:6], refs[6:]
    node, core = position()
    ship_ref = ships[t]
    mine = [note(ref)[16:19] for ref in ships]
    tile = envs[3][0, :HALF, WIDE - LANES :].astype(F32)
    tile = jnp.where(iota((HALF, LANES), 1) >= B, tile, pltpu.roll(tile, B, 1))
    theirs = [tile[0:3], tile[3:6]]
    by_node = []
    for e in range(nodes):
        value = jnp.zeros((1, LANES), F32)
        for sums, c in ((mine, core), (theirs, 1 - core)):
            for hop, p in enumerate(sums):
                source = lax.rem(node + 2 * nodes - 2 * c - hop, nodes)
                value = value + jnp.where(source == e, p[0:1] + p[1:2] + p[2:3], 0.0)
        by_node.append(value)
    squares = (by_node[0] + by_node[1]) + (by_node[2] + by_node[3])
    scale = 1.0 / jnp.sqrt(squares / count + 1e-06)
    scale_ref[...] = jnp.broadcast_to(scale, scale_ref.shape)
    for s in range(q_ref.shape[0]):
        q_ref[s] = ship_ref[HALF * s : HALF * (s + 1), :].astype(F32) * scale
    product(q_ref, envs, y_ref, inner_ref, True)


def orthogonal(ship_ref, own_ref, other_ref, basis, q_ref):
    n = note(ship_ref)
    cap = q_ref.shape[0]
    ahead = lax.axis_index("op") < 2
    own_scales, other_scales = decode_scales(own_ref), decode_scales(other_ref)
    for s in range(cap):
        own, other = decode(own_ref, s, own_scales), decode(other_ref, s, other_scales)
        image = jnp.where(ahead, own, other) + jnp.where(ahead, other, own)
        q_ref[s] = image * inside(n[s : s + 1], n[cap + s : cap + s + 1])
    image = q_ref[...].reshape(cap * HALF, LANES)
    rows = []
    rest = image
    for ref in basis:
        q = ref[...].reshape(cap * HALF, LANES)
        length = total_of(q * q)
        along = total_of(q * image)
        row = wide(jnp.where(length > 0, along / jnp.where(length > 0, length, 1.0), 0.0))
        rest = rest - row * q
        rows.append(row)
    q_ref[...] = rest.reshape(q_ref.shape)
    return rows


def step_kernel(count, *refs):
    ship_ref, own_ref, other_ref = refs[:3]
    basis = refs[3 : 3 + count]
    envs = refs[3 + count : 7 + count]
    q_ref, y_ref, along_ref, *parcel_ref, inner_ref = refs[7 + count :]
    rows = orthogonal(ship_ref, own_ref, other_ref, basis, q_ref)
    along_ref[...] = jnp.concatenate(rows + [jnp.zeros((8 - count, LANES), F32)], axis=0)
    for ref in parcel_ref:
        mine = jnp.where(lax.axis_index("op") < 2, basis[1][...], q_ref[...])
        mine = mine.reshape(-1, LANES).astype(BF16)
        blank = jnp.zeros((ref.shape[0] - mine.shape[0], LANES), BF16)
        ref[...] = jnp.concatenate([mine, blank], axis=0)
    product(q_ref, envs, y_ref, inner_ref, False)


def line_of(values):
    lane = iota((1, LANES), 1)
    line = jnp.zeros((1, LANES), F32)
    for k, value in enumerate(values):
        line = jnp.where(lane == k, value, line)
    return line


def table_kernel(*refs):
    out_refs, table_ref = refs[16:18], refs[18]
    lines = []
    for t in range(2):
        ship_ref, own_ref, other_ref, q0, q1, q2, c1, c2 = refs[8 * t : 8 * t + 8]
        last = orthogonal(ship_ref, own_ref, other_ref, (q0, q1, q2), out_refs[t])
        vectors = [ref[...].reshape(-1, LANES) for ref in (q0, q1, q2, out_refs[t])]
        values = [total_of(vectors[i] * vectors[j]) for i in range(4) for j in range(i, 4)]
        lines.append(line_of(values + [c1[0:1], c2[0:1], c2[1:2]] + last))
    table_ref[...] = jnp.concatenate(lines + [jnp.zeros((6, LANES), F32)], axis=0)


def pack_kernel(table_ref, other_ref, *refs):
    core = position()[1]
    mine, other = table_ref[0:2, :], other_ref[0:2, :]
    lines = jnp.concatenate([jnp.where(core == 0, mine, other), jnp.where(core == 0, other, mine)], axis=0)
    pieces = [v.astype(F32) for v in split_three(lines)]
    tail = jnp.concatenate(pieces + [jnp.zeros((4, LANES), F32)], axis=0).astype(BF16)
    for ref, out_ref in zip(refs[:2], refs[2:]):
        rows = ref.shape[0] * HALF
        out_ref[:rows, :] = ref[...].reshape(rows, LANES).astype(BF16)
        out_ref[rows:, :] = tail


def combine(count, take):
    gram = {}
    row = 0
    for i in range(4):
        for j in range(i, 4):
            gram[i, j] = gram[j, i] = take(row)
            row += 1
    one = jnp.ones_like(gram[0, 0])
    images = [
        [take(10), one, None, None],
        [take(11), take(12), one, None],
        [take(13), take(14), take(15), one],
    ]

    def mean(u, v):
        acc = None
        for i in range(4):
            for j in range(4):
                if u[i] is not None and v[j] is not None:
                    term = u[i] * v[j] * gram[i, j]
                    acc = term if acc is None else acc + term
        return jnp.sum(acc, axis=0, keepdims=True) / count

    basis = [[one, None, None, None]]
    projections = {}
    for k in range(ITERS):
        image = [None] * 4
        for z, parts in zip(basis[k], images):
            for m, v in enumerate(parts):
                if z is not None and v is not None:
                    image[m] = z * v if image[m] is None else image[m] + z * v
        rest = list(image)
        for i in range(k + 1):
            p = mean(basis[i], image)
            projections[i, k] = p
            for m, v in enumerate(basis[i]):
                if v is not None:
                    rest[m] = rest[m] - p * v
        if k + 1 < ITERS:
            scale = 1.0 / jnp.sqrt(mean(rest, rest) + 1e-06)
            basis.append([None if v is None else v * scale for v in rest])
    return projections, rest


def finish_kernel(count, nodes, back_ref, scale_ref, home_ref, *refs):
    early, late, (out_ref, proj_ref) = refs[:8], refs[8:12], refs[12:]
    node, core = position()
    slots = out_ref.shape[0]
    rows = home_ref.shape[0] // 4
    sources = []
    lines = [jnp.zeros((4, LANES), F32) for _ in range(nodes)]
    for k, ref in enumerate(late):
        hop = 2 * (core if k < 2 else 1 - core) + k % 2
        host = lax.rem(node + hop, nodes)
        tail = ref[rows:, :].astype(F32)
        four = tail[0:4] + tail[4:8] + tail[8:12]
        lines = [jnp.where(host == e, four, v) for e, v in enumerate(lines)]
        sources.append((*early[2 * k : 2 * k + 2], ref, host * 4 + hop))
    table = jnp.concatenate(lines, axis=0)
    sets = 4 * nodes
    projections, rest = combine(
        count, lambda k: jnp.broadcast_to(table[:, k : k + 1], (sets, LANES)))
    lines = [line_of([projections.get((i, k), 0.0) for k in range(ITERS)]) for i in range(ITERS)]
    proj_ref[...] = jnp.concatenate(lines, axis=0)[:, :ITERS]
    scale = scale_ref[0:1, :]
    blocks = []
    ahead = lax.axis_index("op") < 2
    for k, (mine_ref, more_ref, last_ref, index) in enumerate(sources):
        mine = iota((sets, LANES), 0) == index
        coeff = [jnp.sum(jnp.where(mine, v, 0.0), axis=0, keepdims=True) for v in rest]
        x = coeff[0] * (home_ref[rows * k : rows * (k + 1), :].astype(F32) * scale)
        here, there = mine_ref[:rows, :].astype(F32), more_ref[:rows, :].astype(F32)
        x = x + coeff[1] * jnp.where(ahead, here, there) + coeff[2] * jnp.where(ahead, there, here)
        x = x + coeff[3] * last_ref[:rows, :].astype(F32)
        blocks.append(x)
    first = back_ref[...]
    second = from_kept_twice()
    per = rows // HALF
    for c in range(4):
        x = jnp.concatenate(
            [blocks[k // per][HALF * (k % per) + 8 * c : HALF * (k % per) + 8 * c + 8] for k in range(slots)],
            axis=0,
        )
        x = jnp.dot(first, jnp.concatenate(split(x), axis=1), preferred_element_type=F32).astype(BF16)
        x = jnp.dot(x, second, preferred_element_type=F32)
        for i in range(8):
            out_ref[:, (8 * c + i) * LANES : (8 * c + i + 1) * LANES] = x[i * slots : (i + 1) * slots]


def paired(start_vector, extents, offsets, env_left, env_right, channel_mask):
    nodes = lax.axis_size("sector")
    ops = lax.axis_size("op")
    slots = start_vector.shape[0]
    cap = slots // nodes
    count = float(slots * nodes * B * B)
    swap_core = [(i, i ^ 1) for i in range(ops)]
    swap_x = [(i, i ^ 2) for i in range(ops)]
    left = jnp.transpose(env_left, (1, 0, 2))
    right = jnp.transpose(env_right, (1, 0, 2))
    meta = jnp.concatenate([offsets[None], jnp.transpose(extents), jnp.transpose(channel_mask)], axis=0)

    def route(t, back):
        pairs = []
        for h in range(nodes):
            for q in range(ops):
                to = (h + 2 * (q % 2) + t) % nodes
                a, b = h * ops + q, to * ops + q
                pairs.append((b, a) if back else (a, b))
        return pairs

    def across(x):
        return lax.ppermute(x, "op", swap_core)

    def shape(dims, dtype=F32):
        return jax.ShapeDtypeStruct(dims, dtype)

    environment = shape((cap, B, WIDE), BF16)
    vector = shape((cap, HALF, LANES))
    tile = shape((8, LANES))
    code = shape((cap * HALF + 16, LANES), jnp.int16)
    payload = shape((cap * HALF + 32, LANES), BF16)
    one_hots = shape((8 * slots, 8 * slots), BF16)
    first, back, *ships, home = call(
        ship_kernel, "ship",
        (one_hots, one_hots, payload, payload, shape((slots * HALF, LANES), BF16)),
        (meta, meta, start_vector), "svv",
        [pltpu.SMEM((slots,), jnp.int32), pltpu.SMEM((nodes,), jnp.int32)], "vvvvv", 2.0, ROOMY, True)
    ships = [lax.ppermute(x, ("sector", "op"), route(t, False)) for t, x in enumerate(ships)]

    def arrange(masked, operands, kinds):
        sets = call(
            lambda *refs: arrange_kernel(masked, *refs), "arrange", (environment,) * 4, operands, kinds,
            cost=3.0, limit=ARRANGE, compute=True)
        return sets[:2], [across(x) for x in sets[2:]]

    keep_left, got_left = arrange(True, (first, left, meta), "vvv")
    ships = call(arrived_kernel, "arrived", (payload, payload), (*ships, keep_left[0]), "vva", cost=0.3)
    keep_right, got_right = arrange(False, (first, right, *ships), "vvvv")
    envs = [(keep_left[t], keep_right[t], got_left[t], got_right[t]) for t in range(2)]

    def step(k):
        return lambda *refs: step_kernel(k, *refs)

    inner = [pltpu.VMEM((cap, LANES, 2 * WIDE), BF16)]
    basis = [[], []]
    along = [[], []]
    images = [None, None]
    early = []
    for t in range(2):
        q, y, scale = call(
            lambda *refs, t=t: start_kernel(count, nodes, t, *refs), "first", (vector, code, tile),
            (*ships, *envs[t]), "v" * 6, inner)
        basis[t].append(q)
        images[t] = (y, lax.ppermute(y, "op", swap_x))
    for k in range(1, ITERS):
        for t in range(2):
            outs = [vector, code, tile]
            if k == ITERS - 1:
                outs.append(shape(code.shape, BF16))
            q, y, a, *parcel = call(
                step(k), ("second", "third")[k - 1], tuple(outs),
                (ships[t], *images[t], *basis[t], *envs[t]), "v" * (7 + k), inner)
            basis[t].append(q)
            along[t].append(a)
            images[t] = (y, lax.ppermute(y, "op", swap_x))
            early += [lax.ppermute(x, ("sector", "op"), route(t, True)) for x in parcel]
    early = [(x, lax.ppermute(x, "op", swap_x)) for x in early]
    early += [tuple(across(x) for x in pair) for pair in early]
    early = [x for pair in early for x in pair]

    operands = []
    for t in range(2):
        operands += [ships[t], *images[t], *basis[t], *along[t]]
    *last, table = call(table_kernel, "table", (vector, vector, tile), operands, "v" * 16, cost=1.0)
    parcel = shape((cap * HALF + 16, LANES), BF16)
    late = call(
        pack_kernel, "pack", (parcel, parcel), (table, across(table), *last), "vvvv", cost=0.7)
    late = [lax.ppermute(x, ("sector", "op"), route(t, True)) for t, x in enumerate(late)]
    late += [across(x) for x in late]

    def finish(*refs):
        finish_kernel(count, nodes, *refs)

    return call(
        finish, "finish", (shape((slots, B * B)), shape((ITERS, ITERS))),
        (back, scale, home, *early, *late), "v" * 15)


def pack_rows(data, index, nodes, cap):
    slots = data.shape[0]
    hit = jnp.arange(nodes * cap, dtype=jnp.int32)[:, None] == index[None, :]
    source = jnp.sum(jnp.where(hit, jnp.arange(slots, dtype=jnp.int32)[None, :], 0), axis=1)
    filled = jnp.any(hit, axis=1)
    rows = jnp.take(data, source, axis=0)
    rows = jnp.where(filled[:, None], rows, jnp.zeros_like(rows))
    return rows.reshape(nodes, cap, data.shape[1])


def unpack_rows(arrived, index):
    flat = arrived.reshape(arrived.shape[0] * arrived.shape[1], arrived.shape[2])
    return jnp.take(flat, index, axis=0)


def general(start_vector, extents, offsets, env_left, env_right, channel_mask):
    nodes = lax.axis_size("sector")
    here_index = lax.axis_index("sector")
    slots = start_vector.shape[0]
    cap = max(1, slots // nodes)
    chans = env_left.shape[1]
    count = float(slots * nodes * B * B)
    slot_ids = jnp.arange(slots, dtype=jnp.int32)
    same = offsets[:, None] == offsets[None, :]
    earlier = slot_ids[None, :] < slot_ids[:, None]
    rank = jnp.sum((same & earlier).astype(jnp.int32), axis=1)
    send_index = (here_index + offsets) % nodes * cap + rank
    recv_index = (here_index - offsets) % nodes * cap + rank
    position = jnp.arange(B * B, dtype=jnp.int32)
    inside = ((position // B)[None, :] < extents[:, 0:1]) & (
        (position % B)[None, :] < extents[:, 1:2]
    )
    mask = inside.astype(jnp.float32)
    left = env_left.reshape(slots, chans, B, B)
    right_wide = env_right.reshape(slots, chans, B, B).astype(jnp.float32)
    chan = channel_mask.astype(jnp.float32)

    def squares(vector):
        return lax.psum(jnp.sum(vector * vector), "sector") / count

    def correlation_table(basis, image):
        local = [jnp.sum(vector * image) for vector in basis]
        local = local + [jnp.zeros((), jnp.float32)] * (ITERS - len(basis))
        return lax.psum(jnp.stack(local), "sector") / count

    masked = mask * start_vector.astype(jnp.float32)
    basis = [masked / jnp.sqrt(squares(masked) + 1e-06)]
    projections = jnp.zeros((ITERS, ITERS), jnp.float32)
    residual = masked
    for step in range(ITERS):
        moving = pack_rows(basis[step].astype(jnp.bfloat16), send_index, nodes, cap)
        arrived = lax.all_to_all(moving, "sector", split_axis=0, concat_axis=0, tiled=True)
        blocks = unpack_rows(arrived, recv_index).reshape(slots, B, B)
        inner = jnp.einsum("swab,sbc->swac", left, blocks, preferred_element_type=jnp.float32)
        inner = inner * chan[:, :, None, None]
        partial_image = jnp.einsum(
            "swac,swdc->sad", inner, right_wide, precision=lax.Precision.HIGHEST
        )
        total = lax.psum(partial_image.reshape(slots, B * B), "op")
        going = pack_rows(total, recv_index, nodes, cap)
        returned = lax.all_to_all(going, "sector", split_axis=0, concat_axis=0, tiled=True)
        apply_image = unpack_rows(returned, send_index)
        image = apply_image * mask
        coeffs = correlation_table(basis, image)
        residual = image
        for index in range(step + 1):
            projections = projections.at[index, step].set(coeffs[index])
            residual = residual - coeffs[index] * basis[index]
        if step + 1 < ITERS:
            basis.append(residual / jnp.sqrt(squares(residual) + 1e-06))
    return (residual, projections)


def solution(mesh):
    def on_device(start_vector, extents, offsets, env_left, env_right, channel_mask):
        nodes, ops = mesh.shape["sector"], mesh.shape["op"]
        slots, chans = env_left.shape[:2]
        fits = nodes == 4 and ops == 4 and slots == 8 * nodes and chans < 8
        body = paired if fits else general
        return body(start_vector, extents, offsets, env_left, env_right, channel_mask)

    return jax.shard_map(
        on_device,
        mesh=mesh,
        in_specs=(
            P(("groups", "sector"), None),
            P(("groups", "sector"), None),
            P("groups"),
            P(("groups", "sector"), "op", None),
            P(("groups", "sector"), "op", None),
            P(("groups", "sector"), "op"),
        ),
        out_specs=(P(("groups", "sector"), None), P("groups", None)),
        check_vma=False,
    )
```
